256 devices in a mesh: dom: 64 (over x, z, core), rep: 4 (over y).
Axes of the slice: x: 4, y: 4, z: 8, core: 2. Of those that a mesh axis runs over, the one named last changes fastest.
Arguments:
- features: bfloat16 [196608, 512], P('dom', 'rep')
- send_rows: int32 [4096, 192], P('dom'), may hold values from 0 to 3071
- neighbours: int32 [196608, 10], P('dom'), may hold values from 0 to 15359
- w_self1: bfloat16 [512, 512], P(None, 'rep'), may hold values from -0.25 to 0.25
- w_neigh1: bfloat16 [512, 512], P(None, 'rep'), may hold values from -0.25 to 0.25
- w_self2: bfloat16 [512, 512], P(None, 'rep'), may hold values from -0.25 to 0.25
- w_neigh2: bfloat16 [512, 512], P(None, 'rep'), may hold values from -0.25 to 0.25
- queries: bfloat16 [16384, 512], P('dom', 'rep'), may hold values from -0.25 to 0.25
- owners: int32 [16384, 4], P('dom'), may hold values from 0 to 63, all different within a row; in each aligned block of 256 rows (0 to 255, 256 to 511, ...) at most 32 rows name the same one
- slate: int32 [16384, 4, 8], P('dom'), may hold values from 0 to 3071
Outputs:
- node_embed: bfloat16 [196608, 512], P('dom', 'rep')
- scores: float32 [16384, 32], P('dom')
The draws below stay inside these ranges and needn't reach their ends.
Inputs may be any that keep to these rules, and one draw needn't show every extreme that they name: `neighbours`: indices below 3072 are the partition's own nodes; index 3072 + s * 192 + r is row r of what partition s sends to this one. `owners`: each row names 4 different partitions; among the rows of one partition no partition is named by more than 32 rows, and that bound is reached.
All inputs are finite; a program needn't handle non-finite values.
Results may differ from the reference program's by a relative error of at most 0.0053.
Values may be sent and summed in bfloat16 or wider, within the bound.
A program may use at most 64 MiB of HBM per device.

```python
import math
import jax
import jax.numpy as jnp
import numpy as np
from jax import lax

F = 512
K = 10
TOPQ = 4
S = 8
NODE_DEV = 3072
HB = 192
Q_DEV = 256
NODES = 196608
Q_TOTAL = 16384
CAP = 32
N_DOM = 64


def draw_features(key, part):
    key = jax.random.fold_in(key, 11)
    key_base, key_scale = jax.random.split(key, 2)
    scales = jnp.exp(jax.random.uniform(key_scale, (NODES, 1), minval=0.0, maxval=math.log(10.0)))
    base = jax.random.normal(key_base, (NODES, F))
    return (base * scales / 3.0).astype(jnp.bfloat16)


def touch_ends(values, rng, least, largest):
    index_at = [jax.random.randint(jax.random.fold_in(rng, axis), (), 0, length) for axis, length in enumerate(values.shape)]
    longest = values.shape.index(max(values.shape))
    beside = index_at[:longest] + [(index_at[longest] + 1) % values.shape[longest]] + index_at[longest + 1:]
    return values.at[tuple(index_at)].set(least).at[tuple(beside)].set(largest)


def level_of(own_key, shape, cuts, low, top_value):
    def one(axis_at, blocks):
        steps = jax.random.uniform(jax.random.fold_in(jax.random.fold_in(own_key, 6), axis_at), (blocks,), jnp.float32, low / len(cuts), top_value / len(cuts))
        return jnp.repeat(jnp.exp(steps), shape[axis_at] // blocks).reshape((-1,) + (1,) * (len(shape) - axis_at - 1))

    gain = one(*cuts[0])
    for cut in cuts[1:]:
        gain = gain * one(*cut)
    return gain


def assign_block(key, own, number, rows, number_of, top, reach, lean):
    ranking = jax.random.permutation(key, number_of)
    packed, common = shares(number_of, rows * top, reach, lean, True), shares(number_of, rows * top, reach, lean, False)
    places = jnp.arange(number_of)

    def named(sizes, offset_by):
        used = int((sizes > 0).sum())
        fixed = max(1, used // 4)
        passed = fixed + (places - fixed + offset_by * (used - fixed)) % max(1, number_of - fixed)
        return jnp.zeros((number_of,), jnp.int32).at[ranking[jnp.where(places < fixed, places, passed)]].set(jnp.asarray(sizes, jnp.int32))

    sizes = jnp.where(number % 4 == 0, named(packed, number // 4), named(common, number - number // 4 - 1))
    mixed = jax.random.permutation(jax.random.fold_in(own, 3), number_of)
    source_of, sink = mixed[0:number_of // 2 * 2:2], mixed[1:number_of // 2 * 2:2]
    slack = jnp.minimum(sizes[source_of] - 1, reach - sizes[sink]) // 2
    slack = jnp.where((source_of == ranking[0]) | (sink == ranking[0]) | (sizes[sink] == 0), 0, jnp.maximum(slack, 0))
    passed = jax.random.randint(jax.random.fold_in(own, 4), (number_of // 2,), 0, 1 << 20) % (slack + 1)
    sizes = sizes.at[source_of].add(-passed).at[sink].add(passed)
    items = jnp.searchsorted(jnp.cumsum(sizes), jnp.arange(rows * top), side="right").astype(jnp.int32)
    grid = items.reshape(top, rows).T
    grid = grid[jax.random.permutation(jax.random.fold_in(own, 1), rows)]
    offset_by = jax.random.randint(jax.random.fold_in(own, 2), (rows, 1), 0, top)
    return jnp.take_along_axis(grid, (jnp.arange(top)[None, :] + offset_by) % top, axis=1)


def shares(count, total, bound, slope, full):
    loads = [(1 << 20) // math.isqrt(grade ** slope) + 1 for grade in range(1, count + 1)]
    largest = bound if full else min(bound, max(-(-total // count), total * loads[0] // sum(loads)))
    least = 1 if total - largest >= count - 1 else 0
    given, surplus = [largest] + [least] * (count - 1), total - largest - least * (count - 1)
    while surplus > 0:
        free = [i for i in range(1, count) if given[i] < largest] or [i for i in range(1, count) if given[i] < bound]
        pool, budget = sum([loads[i] for i in free]), surplus
        for i in free:
            addition = min(bound - given[i], max(1, budget * loads[i] // pool), surplus)
            given[i] = given[i] + addition
            surplus = surplus - addition
    return np.array(given)


def bell_draw(own_key, extent, spread, reach, pieces=(), kind=jnp.bfloat16):
    level = level_of(own_key, extent, pieces, -0.22, 0.18) if pieces else 1.0
    entries = jax.random.normal(own_key, extent, jnp.float32) * spread * level
    return jnp.minimum(jnp.maximum(entries, -reach), reach).astype(kind)


def setup_inputs(seed: int = 0) -> dict:
    arg_keys = jax.random.split(jax.random.key(seed), 11)
    features = draw_features(jax.random.fold_in(arg_keys[10], 71), 0)
    send_rows = touch_ends(jax.random.randint(arg_keys[1], (N_DOM * N_DOM, HB), 0, NODE_DEV), jax.random.fold_in(arg_keys[1], 1), 0, NODE_DEV - 1).astype(jnp.int32)
    neighbours = touch_ends(jax.random.randint(arg_keys[2], (NODES, K), 0, NODE_DEV + N_DOM * HB), jax.random.fold_in(arg_keys[2], 1), 0, (NODE_DEV + N_DOM * HB) - 1).astype(jnp.int32)
    w_self1 = bell_draw(arg_keys[3], (F, F), F ** -0.5, 0.25, ((1, 4),))
    w_neigh1 = bell_draw(arg_keys[4], (F, F), F ** -0.5, 0.25, ((1, 4),))
    w_self2 = bell_draw(arg_keys[5], (F, F), F ** -0.5, 0.25, ((1, 4),))
    w_neigh2 = bell_draw(arg_keys[6], (F, F), F ** -0.5, 0.25, ((1, 4),))
    queries = bell_draw(arg_keys[7], (Q_TOTAL, F), F ** -0.5, 0.25, ((0, 64), (1, 4)))
    owners_keys = jax.random.split(jax.random.fold_in(arg_keys[8], 1), Q_TOTAL // Q_DEV)
    owners_turns = jax.random.permutation(jax.random.fold_in(arg_keys[8], 3), Q_TOTAL // Q_DEV)
    owners = jax.vmap(lambda own, number: assign_block(jax.random.fold_in(arg_keys[8], 2), own, number, Q_DEV, N_DOM, TOPQ, CAP, 2))(owners_keys, owners_turns).reshape((Q_TOTAL, TOPQ))
    slate = touch_ends(jax.random.randint(arg_keys[9], (Q_TOTAL, TOPQ, S), 0, NODE_DEV), jax.random.fold_in(arg_keys[9], 1), 0, NODE_DEV - 1).astype(jnp.int32)
    return dict(features=features, send_rows=send_rows, neighbours=neighbours, w_self1=w_self1, w_neigh1=w_neigh1, w_self2=w_self2, w_neigh2=w_neigh2, queries=queries, owners=owners, slate=slate)


def sage_block(h_rows, neighbour_rows, table, w_self, w_neigh, active):
    agg = (lax.optimization_barrier(jnp.sum(table[neighbour_rows], axis=1, dtype=jnp.float32)) / K).astype(jnp.bfloat16)
    z = jnp.dot(h_rows, w_self, preferred_element_type=jnp.float32) + jnp.dot(agg, w_neigh, preferred_element_type=jnp.float32)
    if active:
        z = jax.nn.relu(z)
    scale = lax.rsqrt(lax.optimization_barrier(jnp.mean(z * z, axis=1, keepdims=True)) + 1e-06)
    return (z * scale).astype(jnp.bfloat16)

def reference(features, send_rows, neighbours, w_self1, w_neigh1, w_self2, w_neigh2, queries, owners, slate):
    nodes = features.shape[0]
    partition = (jnp.arange(nodes, dtype=jnp.int32) // NODE_DEV)[:, None]
    local_ids = neighbours < NODE_DEV
    offset = jnp.maximum(neighbours - NODE_DEV, 0)
    source = offset // HB
    within = offset % HB
    remote_rows = send_rows[source * N_DOM + partition, within]
    global_ids = jnp.where(local_ids, partition * NODE_DEV + neighbours, source * NODE_DEV + remote_rows).astype(jnp.int32)
    blocked_ids = global_ids.reshape(N_DOM, NODE_DEV, K)

    def layer(h, w_self, w_neigh, active):
        blocks = h.reshape(N_DOM, NODE_DEV, F)
        out = lax.map(lambda pair: sage_block(pair[0], pair[1], h, w_self, w_neigh, active), (blocks, blocked_ids))
        return out.reshape(nodes, F)
    hidden_one = layer(features, w_self1, w_neigh1, True)
    node_embed = layer(hidden_one, w_self2, w_neigh2, False)
    item_ids = (owners[:, :, None] * NODE_DEV + slate).astype(jnp.int32)
    query_blocks = queries.reshape(N_DOM, Q_DEV, F)
    id_blocks = item_ids.reshape(N_DOM, Q_DEV, TOPQ, S)

    def score_block(pair):
        items = node_embed[pair[1]].astype(jnp.float32)
        return jnp.einsum('qf,qtsf->qts', pair[0].astype(jnp.float32), items)
    scores = lax.map(score_block, (query_blocks, id_blocks))
    return (node_embed, scores.reshape(N_DOM * Q_DEV, TOPQ * S))
```

```python
import functools

import jax
import jax.numpy as jnp
from jax import lax
from jax.experimental import pallas as pl
from jax.experimental.pallas import tpu as pltpu
from jax.sharding import PartitionSpec as P

MESH = pl.DeviceIdType.MESH
VMEM = pltpu.VMEM
F32 = jnp.float32
BF16 = jnp.bfloat16
LANE = 128
EPS = 1e-06


def rep_barrier(me, nrep):
    barrier = pltpu.get_barrier_semaphore()
    for step in range(1, nrep):
        pl.semaphore_signal(
            barrier, inc=1, device_id={"rep": lax.rem(me + step, nrep)}, device_id_type=MESH
        )
    pl.semaphore_wait(barrier, nrep - 1)


def columns_of(which):
    return pl.ds(pl.multiple_of(which * LANE, LANE), LANE)


def rows_of(which, count):
    return pl.ds(pl.multiple_of(which * count, count), count)


def pick_rows(index_ref, start, table, stage, count, unroll):
    def some(block, carry):
        base = block * unroll
        for u in range(unroll):
            stage[pl.ds(base + u, 1), :] = table[pl.ds(index_ref[start + base + u], 1), :]
        return carry

    lax.fori_loop(0, count // unroll, some, 0)


def send_gather(index_ref, table, stage, out_ref, parts, unroll):
    count = stage.shape[0]

    def part(p, carry):
        pick_rows(index_ref, p * count, table, stage, count, unroll)
        out_ref[rows_of(p, count), :] = stage[...].astype(BF16)
        return carry

    lax.fori_loop(0, parts, part, 0)


def sum_rows(index_ref, start, table, stage, nodes, fan, unroll):
    def some(block, carry):
        base = block * unroll
        for u in range(unroll):
            terms = [
                table[pl.ds(index_ref[k * nodes + start + base + u], 1), :] for k in range(fan)
            ]
            while len(terms) > 1:
                pairs = [terms[i] + terms[i + 1] for i in range(0, len(terms) - 1, 2)]
                terms = pairs + terms[len(pairs) * 2 :]
            stage[pl.ds(base + u, 1), :] = terms[0]
        return carry

    lax.fori_loop(0, stage.shape[0] // unroll, some, 0)


def first_kernel(nrep, ndom, send_idx, own, out_rows, outgoing, table, stage, send, recv, local):
    me = lax.axis_index("rep")
    chunk = own.shape[0] // nrep
    rep_barrier(me, nrep)
    copies = []
    for step in range(nrep - 1):
        to = lax.rem(me + 1 + step, nrep)
        copy = pltpu.make_async_remote_copy(
            src_ref=own.at[rows_of(to, chunk), :],
            dst_ref=out_rows.at[:, columns_of(me)],
            send_sem=send.at[step],
            recv_sem=recv.at[step],
            device_id={"rep": to},
            device_id_type=MESH,
        )
        copy.start()
        copies.append(copy)
    mine = pltpu.make_async_copy(
        own.at[rows_of(me, chunk), :], out_rows.at[:, columns_of(me)], local.at[0]
    )
    mine.start()
    table[...] = own[...].astype(F32)
    send_gather(send_idx, table, stage, outgoing, ndom, 32)
    mine.wait()
    for copy in copies:
        copy.wait()


def layer_core(
    nrep, fan, active, neigh_idx, own, incoming, self_rows, weights,
    hid_rows, hid_cols, table, stage, chunks, agg_rows, send, recv, hsend, hrecv, local,
):
    me = lax.axis_index("rep")
    nodes = own.shape[0]
    chunk = nodes // nrep
    width = self_rows.shape[1]
    rep_barrier(me, nrep)
    table[pl.ds(0, nodes), :] = own[...].astype(F32)
    table[pl.ds(nodes, incoming.shape[0]), :] = incoming[...].astype(F32)
    copies = []
    for step in range(nrep):
        to = lax.rem(me + 1 + step, nrep)
        sum_rows(neigh_idx, to * chunk, table, stage, nodes, fan, 16)
        chunks[step] = (stage[...] / fan).astype(BF16)
        if step < nrep - 1:
            copy = pltpu.make_async_remote_copy(
                src_ref=chunks.at[step],
                dst_ref=agg_rows.at[:, columns_of(me)],
                send_sem=send.at[step],
                recv_sem=recv.at[step],
                device_id={"rep": to},
                device_id_type=MESH,
            )
        else:
            copy = pltpu.make_async_copy(
                chunks.at[step], agg_rows.at[:, columns_of(me)], local.at[0]
            )
        copy.start()
        copies.append(copy)
    for copy in copies:
        copy.wait()
    tiles = hsend.shape[0]
    tile = chunk // tiles
    back = []
    for t in range(tiles):
        rows = pl.ds(t * tile, tile)
        z = jnp.dot(self_rows[rows, :], weights[pl.ds(0, width), :], preferred_element_type=F32)
        z = z + jnp.dot(
            agg_rows[rows, :], weights[pl.ds(width, width), :], preferred_element_type=F32
        )
        if active:
            z = jnp.maximum(z, 0.0)
        mean = jnp.sum(z * z, axis=1, keepdims=True) / width
        hid_rows[rows, :] = (z * lax.rsqrt(mean + EPS)).astype(BF16)
        landing = pl.ds(pl.multiple_of(me * chunk + t * tile, tile), tile)
        for step in range(nrep - 1):
            to = lax.rem(me + 1 + step, nrep)
            copy = pltpu.make_async_remote_copy(
                src_ref=hid_rows.at[rows, columns_of(to)],
                dst_ref=hid_cols.at[landing, :],
                send_sem=hsend.at[t, step],
                recv_sem=hrecv.at[t, step],
                device_id={"rep": to},
                device_id_type=MESH,
            )
            copy.start()
            back.append(copy)
        copy = pltpu.make_async_copy(
            hid_rows.at[rows, columns_of(me)], hid_cols.at[landing, :], local.at[1 + t]
        )
        copy.start()
        back.append(copy)
    for copy in back:
        copy.wait()
    table[pl.ds(0, nodes), :] = hid_cols[...].astype(F32)


def middle_kernel(
    nrep, ndom, fan, neigh_idx, send_idx, own, incoming, self_rows, weights,
    hid_rows, hid_cols, outgoing, table, stage, pick, chunks, agg_rows, *sems,
):
    layer_core(
        nrep, fan, True, neigh_idx, own, incoming, self_rows, weights,
        hid_rows, hid_cols, table, stage, chunks, agg_rows, *sems,
    )
    send_gather(send_idx, table, pick, outgoing, ndom, 32)


def last_kernel(
    nrep, ndom, fan, neigh_idx, items, own, incoming, self_rows, weights, queries,
    hid_cols, scores, table, stage, pick, chunks, agg_rows, hid_rows, partial, psend, precv, *sems,
):
    me = lax.axis_index("rep")
    layer_core(
        nrep, fan, False, neigh_idx, own, incoming, self_rows, weights,
        hid_rows, hid_cols, table, stage, chunks, agg_rows, *sems,
    )
    count = pick.shape[0]
    slots = queries.shape[0] // ndom
    owns = lax.broadcasted_iota(jnp.int32, (slots, count), 0)
    slot = lax.rem(lax.broadcasted_iota(jnp.int32, (slots, count), 1), slots)

    def part(p, carry):
        pick_rows(items, p * count, table, pick, count, 32)
        products = lax.dot_general(
            queries[rows_of(p, slots), :],
            pick[...].astype(BF16),
            (((1,), (1,)), ((), ())),
            preferred_element_type=F32,
        )
        partial[me, pl.ds(p, 1), :] = jnp.sum(
            jnp.where(owns == slot, products, 0.0), axis=0, keepdims=True
        )
        return carry

    lax.fori_loop(0, ndom, part, 0)
    copies = []
    for step in range(nrep - 1):
        copy = pltpu.make_async_remote_copy(
            src_ref=partial.at[me],
            dst_ref=partial.at[me],
            send_sem=psend.at[step],
            recv_sem=precv.at[step],
            device_id={"rep": lax.rem(me + 1 + step, nrep)},
            device_id_type=MESH,
        )
        copy.start()
        copies.append(copy)
    for copy in copies:
        copy.wait()
    total = partial[0]
    for other in range(1, nrep):
        total = total + partial[other]
    scores[...] = total


def call(kernel, name, number, outs, scratch, smem, args):
    whole = pl.BlockSpec(memory_space=VMEM)
    return pl.pallas_call(
        kernel,
        out_shape=outs,
        in_specs=[pl.BlockSpec(memory_space=pltpu.SMEM)] * smem + [whole] * (len(args) - smem),
        out_specs=[whole] * len(outs),
        scratch_shapes=scratch,
        compiler_params=pltpu.CompilerParams(
            collective_id=number, has_side_effects=True, vmem_limit_bytes=44 * 1024 * 1024
        ),
        name=name,
    )(*args)


def body(
    features, send_rows, neighbours, w_self1, w_neigh1, w_self2, w_neigh2, queries, owners, slate
):
    ndom, nrep = lax.axis_size("dom"), lax.axis_size("rep")
    nodes, width = features.shape
    fan = neighbours.shape[1]
    per_pair = send_rows.shape[1]
    chunk = nodes // nrep
    full = width * nrep
    sessions, topq, nitems = slate.shape
    capacity = min(sessions, 2 * sessions * topq // ndom)
    entries, nslots = sessions * topq, ndom * capacity
    count = capacity * nitems
    tiles = 3
    dma = pltpu.SemaphoreType.DMA

    send_idx = send_rows.reshape(-1)
    neigh_idx = neighbours.T.reshape(-1)
    weights1 = lax.all_gather(jnp.concatenate([w_self1, w_neigh1], 0), "rep", axis=1, tiled=True)
    weights2 = lax.all_gather(jnp.concatenate([w_self2, w_neigh2], 0), "rep", axis=1, tiled=True)

    shape = jax.ShapeDtypeStruct
    x_rows, outgoing = call(
        functools.partial(first_kernel, nrep, ndom),
        "send_gather",
        1,
        [shape((chunk, full), BF16), shape((ndom * per_pair, width), BF16)],
        [
            VMEM((nodes, width), F32),
            VMEM((per_pair, width), F32),
            dma((nrep - 1,)),
            dma((nrep - 1,)),
            dma((1,)),
        ],
        1,
        [send_idx, features],
    )

    def exchange(rows):
        rows = rows.reshape(ndom, per_pair, width)
        rows = lax.all_to_all(rows, "dom", split_axis=0, concat_axis=0, tiled=True)
        return rows.reshape(ndom * per_pair, width)

    incoming = exchange(outgoing)

    owner_of = owners.T.reshape(entries)
    named = owner_of[:, None] == jnp.arange(ndom, dtype=jnp.int32)[None, :]
    order = jnp.arange(entries, dtype=jnp.int32)
    earlier = (order[:, None] > order[None, :]).astype(BF16)
    before = jnp.dot(earlier, named.astype(BF16), preferred_element_type=F32)
    position = jnp.sum(jnp.where(named, before, 0.0), axis=1).astype(jnp.int32)
    slot_index = owner_of * capacity + position
    place = (jnp.arange(nslots, dtype=jnp.int32)[:, None] == slot_index[None, :]).astype(BF16)
    slot_queries = jnp.dot(place, jnp.tile(queries, (topq, 1)), preferred_element_type=F32)
    slot_queries = slot_queries.astype(BF16).reshape(ndom, capacity, width)
    lists = slate.transpose(1, 0, 2).reshape(entries, nitems)
    digits = jnp.concatenate([lists // 64, lists % 64], axis=1).astype(BF16)
    slot_digits = jnp.dot(place, digits, preferred_element_type=F32).astype(BF16)
    slot_digits = slot_digits.reshape(ndom, capacity * 2 * nitems // width, width)
    sent = jnp.concatenate([slot_queries, slot_digits], axis=1)
    got = lax.all_to_all(sent, "dom", split_axis=0, concat_axis=0, tiled=True)
    got_queries = got[:, :capacity].reshape(nslots, width)
    got_digits = got[:, capacity:].reshape(ndom, capacity, 2, nitems).astype(jnp.int32)
    items = (got_digits[:, :, 0] * 64 + got_digits[:, :, 1]).transpose(0, 2, 1).reshape(-1)

    table = VMEM((nodes + ndom * per_pair, width), F32)
    stage = VMEM((chunk, width), F32)
    chunks = VMEM((nrep, chunk, width), BF16)
    agg_rows = VMEM((chunk, full), BF16)
    hid_rows = VMEM((chunk, full), BF16)
    sems = [
        dma((nrep - 1,)),
        dma((nrep - 1,)),
        dma((tiles, nrep - 1)),
        dma((tiles, nrep - 1)),
        dma((1 + tiles,)),
    ]
    h_rows, h_cols, outgoing = call(
        functools.partial(middle_kernel, nrep, ndom, fan),
        "layer_one",
        2,
        [
            shape((chunk, full), BF16),
            shape((nodes, width), BF16),
            shape((ndom * per_pair, width), BF16),
        ],
        [table, stage, VMEM((per_pair, width), F32), chunks, agg_rows] + sems,
        2,
        [neigh_idx, send_idx, features, incoming, x_rows, weights1],
    )
    incoming = exchange(outgoing)
    node_embed, slot_scores = call(
        functools.partial(last_kernel, nrep, ndom, fan),
        "layer_two",
        3,
        [shape((nodes, width), BF16), shape((ndom, count), F32)],
        [table, stage, VMEM((count, width), F32), chunks, agg_rows, hid_rows]
        + [VMEM((nrep, ndom, count), F32), dma((nrep - 1,)), dma((nrep - 1,))]
        + sems,
        2,
        [neigh_idx, items, h_cols, incoming, h_rows, weights2, got_queries],
    )
    fetched = lax.all_to_all(slot_scores, "dom", split_axis=0, concat_axis=0, tiled=True)
    fetched = fetched.reshape(ndom, nitems, capacity).transpose(0, 2, 1).reshape(nslots, nitems)
    scores = fetched[slot_index].reshape(topq, sessions, nitems)
    return (node_embed, scores.transpose(1, 0, 2).reshape(sessions, topq * nitems))


def solution(mesh):
    placed = (
        P("dom", "rep"),
        P("dom", None),
        P("dom", None),
        P(None, "rep"),
        P(None, "rep"),
        P(None, "rep"),
        P(None, "rep"),
        P("dom", "rep"),
        P("dom", None),
        P("dom", None, None),
    )
    return jax.shard_map(
        body,
        mesh=mesh,
        in_specs=placed,
        out_specs=(P("dom", "rep"), P("dom", None)),
        check_vma=False,
    )
```

```python
import functools

import jax
import jax.numpy as jnp
from jax import lax
from jax.experimental import pallas as pl
from jax.experimental.pallas import tpu as pltpu
from jax.sharding import PartitionSpec as P

MESH = pl.DeviceIdType.MESH
VMEM = pltpu.VMEM
F32 = jnp.float32
BF16 = jnp.bfloat16
LANE = 128
EPS = 1e-06
TILES = 3


def columns_of(which):
    return pl.ds(pl.multiple_of(which * LANE, LANE), LANE)


def rows_of(which, count):
    return pl.ds(pl.multiple_of(which * count, count), count)


class Ring:
    def __init__(self, ndom, nx, nz):
        self.ndom, self.nx, self.nz = ndom, nx, nz
        me = lax.axis_index("dom")
        self.me = me
        self.core = lax.rem(me, 2)
        self.z = lax.rem(lax.div(me, 2), nz)
        self.x = lax.div(me, 2 * nz)

    def offset(self, n):
        nz, nx = self.nz, self.nx
        i = lax.rem(n, nz)
        dz = nz // 2 + (1 - 2 * lax.rem(i, 2)) * lax.div(i + 1, 2)
        turn = lax.div(n, nz)
        return lax.rem(lax.div(turn, 2) + 1, nx), dz, 1 - lax.rem(turn, 2)

    def target(self, n):
        dx, dz, dc = self.offset(n)
        x = lax.rem(self.x + dx, self.nx)
        z = lax.rem(self.z + dz, self.nz)
        return (x * self.nz + z) * 2 + lax.rem(self.core + dc, 2)

    def source(self, n):
        dx, dz, dc = self.offset(n)
        x = lax.rem(self.x - dx + self.nx, self.nx)
        z = lax.rem(self.z - dz + self.nz, self.nz)
        return (x * self.nz + z) * 2 + lax.rem(self.core + dc, 2)


def to_dom(src, dst, send, recv, target):
    return pltpu.make_async_remote_copy(
        src_ref=src, dst_ref=dst, send_sem=send, recv_sem=recv,
        device_id={"dom": target}, device_id_type=MESH,
    )


def to_rep(src, dst, send, recv, target):
    return pltpu.make_async_remote_copy(
        src_ref=src, dst_ref=dst, send_sem=send, recv_sem=recv,
        device_id={"rep": target}, device_id_type=MESH,
    )


def pick_rows(index_of, table, stage, unroll):
    def some(block, carry):
        base = block * unroll
        for u in range(unroll):
            stage[pl.ds(base + u, 1), :] = table[pl.ds(index_of(base, u), 1), :]
        return carry

    lax.fori_loop(0, stage.shape[0] // unroll, some, 0)


def sum_rows(index_ref, start, table, stage, nodes, fan, unroll):
    def some(block, carry):
        base = block * unroll
        for u in range(unroll):
            terms = [
                table[pl.ds(index_ref[k * nodes + start + base + u], 1), :] for k in range(fan)
            ]
            while len(terms) > 1:
                pairs = [terms[i] + terms[i + 1] for i in range(0, len(terms) - 1, 2)]
                terms = pairs + terms[len(pairs) * 2 :]
            stage[pl.ds(base + u, 1), :] = terms[0]
        return carry

    lax.fori_loop(0, stage.shape[0] // unroll, some, 0)


def start_boundary(ring, send_idx, table, nodes, pick, outgoing, landing, send, recv):
    count = pick.shape[0]

    def one(n, carry):
        to = ring.target(n)
        pick_rows(lambda base, u: send_idx[to * count + base + u], table, pick, 32)
        outgoing[rows_of(to, count), :] = pick[...].astype(BF16)
        to_dom(
            outgoing.at[rows_of(to, count), :],
            landing.at[rows_of(ring.me, count), :],
            send.at[n],
            recv.at[n],
            to,
        ).start()
        return carry

    lax.fori_loop(0, ring.ndom - 1, one, 0)
    me = ring.me
    pick_rows(lambda base, u: send_idx[me * count + base + u], table, pick, 32)
    table[pl.ds(pl.multiple_of(nodes + me * count, 64), count), :] = pick[...]


def finish_boundary(ring, table, nodes, count, outgoing, landing, send, recv):
    def one(n, carry):
        to, source = ring.target(n), ring.source(n)
        copy = to_dom(
            outgoing.at[rows_of(to, count), :],
            landing.at[rows_of(source, count), :],
            send.at[n],
            recv.at[n],
            to,
        )
        copy.wait_recv()
        table[pl.ds(pl.multiple_of(nodes + source * count, 64), count), :] = landing[
            rows_of(source, count), :
        ].astype(F32)
        copy.wait_send()
        return carry

    lax.fori_loop(0, ring.ndom - 1, one, 0)


def layer(
    active, me, nrep, fan, neigh_idx, nodes, table, stage, before_product,
    self_rows, weights, chunks, agg_rows, hid_rows, hid_cols, send, recv, hsend, hrecv, local,
):
    chunk = nodes // nrep
    width = self_rows.shape[1]
    copies = []
    for step in range(nrep):
        to = lax.rem(me + 1 + step, nrep)
        sum_rows(neigh_idx, to * chunk, table, stage, nodes, fan, 16)
        chunks[step] = (stage[...] / fan).astype(BF16)
        there = agg_rows.at[:, columns_of(me)]
        if step < nrep - 1:
            copy = to_rep(chunks.at[step], there, send.at[step], recv.at[step], to)
        else:
            copy = pltpu.make_async_copy(chunks.at[step], there, local.at[0])
        copy.start()
        copies.append(copy)
    for copy in before_product + copies:
        copy.wait()
    tile = chunk // TILES
    back = []
    for t in range(TILES):
        rows = pl.ds(t * tile, tile)
        z = jnp.dot(self_rows[rows, :], weights[pl.ds(0, width), :], preferred_element_type=F32)
        z = z + jnp.dot(
            agg_rows[rows, :], weights[pl.ds(width, width), :], preferred_element_type=F32
        )
        if active:
            z = jnp.maximum(z, 0.0)
        mean = jnp.sum(z * z, axis=1, keepdims=True) / width
        hid_rows[rows, :] = (z * lax.rsqrt(mean + EPS)).astype(BF16)
        there = hid_cols.at[pl.ds(pl.multiple_of(me * chunk + t * tile, tile), tile), :]
        for step in range(nrep - 1):
            to = lax.rem(me + 1 + step, nrep)
            copy = to_rep(
                hid_rows.at[rows, columns_of(to)], there, hsend.at[t, step], hrecv.at[t, step], to
            )
            copy.start()
            back.append(copy)
        copy = pltpu.make_async_copy(hid_rows.at[rows, columns_of(me)], there, local.at[1 + t])
        copy.start()
        back.append(copy)
    for copy in back:
        copy.wait()
    table[pl.ds(0, nodes), :] = hid_cols[...].astype(F32)


def kernel(
    nrep, ndom, nx, nz, fan, nitems,
    neigh_idx, send_idx, own, wself1, wneigh1, wself2, wneigh2, asked, lists,
    embed, fetched,
    table, stage, pick, found, outgoing, landing1, landing2, chunks1, chunks2, agg1, agg2,
    x_rows, h_rows, e_rows, h_cols, weights1, weights2, got, got_lists, items, partial, total,
    bsend1, brecv1, bsend2, brecv2, qsend, qrecv, isend, irecv, fsend, frecv, xsend, xrecv, wsend, wrecv,
    psend, precv, asend1, arecv1, hsend1, hrecv1, local1, asend2, arecv2, hsend2, hrecv2, local2,
    local,
):
    ring = Ring(ndom, nx, nz)
    me = lax.axis_index("rep")
    nodes = own.shape[0]
    chunk = nodes // nrep
    full = h_rows.shape[1]

    barrier = pltpu.get_barrier_semaphore()

    def greet(n, carry):
        pl.semaphore_signal(barrier, inc=1, device_id={"dom": ring.target(n)}, device_id_type=MESH)
        return carry

    lax.fori_loop(0, ndom - 1, greet, 0)
    for step in range(1, nrep):
        pl.semaphore_signal(
            barrier, inc=1, device_id={"rep": lax.rem(me + step, nrep)}, device_id_type=MESH
        )
    table[pl.ds(0, nodes), :] = own[...].astype(F32)
    pl.semaphore_wait(barrier, ndom - 1 + nrep - 1)

    early = []
    blocks = (
        (wself1, weights1, 0), (wneigh1, weights1, full),
        (wself2, weights2, 0), (wneigh2, weights2, full),
    )
    for step in range(nrep - 1):
        to = lax.rem(me + 1 + step, nrep)
        early.append(
            to_rep(own.at[rows_of(to, chunk), :], x_rows.at[:, columns_of(me)],
                   xsend.at[step], xrecv.at[step], to)
        )
        for b, (part, whole, at) in enumerate(blocks):
            early.append(
                to_rep(part, whole.at[pl.ds(at, full), columns_of(me)],
                       wsend.at[b, step], wrecv.at[b, step], to)
            )
    early.append(
        pltpu.make_async_copy(own.at[rows_of(me, chunk), :], x_rows.at[:, columns_of(me)], local.at[0])
    )
    for b, (part, whole, at) in enumerate(blocks):
        early.append(
            pltpu.make_async_copy(part, whole.at[pl.ds(at, full), columns_of(me)], local.at[1 + b])
        )
    for copy in early:
        copy.start()

    count = pick.shape[0]
    start_boundary(ring, send_idx, table, nodes, pick, outgoing, landing1, bsend1, brecv1)
    finish_boundary(ring, table, nodes, count, outgoing, landing1, bsend1, brecv1)

    qrows = got.shape[0] // ndom
    own_asked = [
        pltpu.make_async_copy(
            asked.at[rows_of(ring.me, qrows), :], got.at[rows_of(ring.me, qrows), :],
            local.at[1 + len(blocks)],
        ),
        pltpu.make_async_copy(
            lists.at[ring.me], got_lists.at[ring.me], local.at[2 + len(blocks)]
        ),
    ]
    for copy in own_asked:
        copy.start()

    def query_copies(n, origin):
        to = ring.target(n)
        return (
            to_dom(asked.at[rows_of(to, qrows), :], got.at[rows_of(origin, qrows), :],
                   qsend.at[n], qrecv.at[n], to),
            to_dom(lists.at[to], got_lists.at[origin], isend.at[n], irecv.at[n], to),
        )

    def ask(n, carry):
        for copy in query_copies(n, ring.me):
            copy.start()
        return carry

    lax.fori_loop(0, ndom - 1, ask, 0)
    layer(
        True, me, nrep, fan, neigh_idx, nodes, table, stage, early, x_rows, weights1,
        chunks1, agg1, h_rows, h_cols, asend1, arecv1, hsend1, hrecv1, local1,
    )
    start_boundary(ring, send_idx, table, nodes, pick, outgoing, landing2, bsend2, brecv2)

    def asked_by(n, carry):
        for copy in query_copies(n, ring.source(n)):
            copy.wait()
        return carry

    lax.fori_loop(0, ndom - 1, asked_by, 0)
    for copy in own_asked:
        copy.wait()
    into = pltpu.make_async_copy(got_lists, items, local.at[3 + len(blocks)])
    into.start()
    into.wait()
    finish_boundary(ring, table, nodes, count, outgoing, landing2, bsend2, brecv2)
    layer(
        False, me, nrep, fan, neigh_idx, nodes, table, stage, [], h_rows, weights2,
        chunks2, agg2, e_rows, embed, asend2, arecv2, hsend2, hrecv2, local2,
    )

    slots = qrows
    half = got_lists.shape[1]
    wide = found.shape[0]
    owns = lax.broadcasted_iota(jnp.int32, (slots, wide), 0)
    slot = lax.rem(lax.broadcasted_iota(jnp.int32, (slots, wide), 1), slots)

    def score(p, carry):
        for h in range(half):
            pick_rows(
                lambda base, u: items[p, h, base + u],
                table, found.at[pl.ds(h * LANE, LANE), :], 32,
            )
        products = lax.dot_general(
            got[pl.ds(pl.multiple_of(p * qrows, 16), slots), :],
            found[...].astype(BF16),
            (((1,), (1,)), ((), ())),
            preferred_element_type=F32,
        )
        kept = jnp.sum(jnp.where(owns == slot, products, 0.0), axis=0, keepdims=True)
        for h in range(half):
            partial[me, p, pl.ds(h, 1), :] = kept[:, h * LANE : (h + 1) * LANE]
        return carry

    lax.fori_loop(0, ndom, score, 0)
    copies = []
    for step in range(nrep - 1):
        copy = to_rep(partial.at[me], partial.at[me], psend.at[step], precv.at[step],
                      lax.rem(me + 1 + step, nrep))
        copy.start()
        copies.append(copy)
    for copy in copies:
        copy.wait()
    added = partial[0]
    for other in range(1, nrep):
        added = added + partial[other]
    total[...] = added
    fetched[ring.me] = total[ring.me]

    def answer(n, carry):
        to = ring.target(n)
        to_dom(total.at[to], fetched.at[ring.me], fsend.at[n], frecv.at[n], to).start()
        return carry

    def answered(n, carry):
        to, source = ring.target(n), ring.source(n)
        to_dom(total.at[to], fetched.at[source], fsend.at[n], frecv.at[n], to).wait()
        return carry

    lax.fori_loop(0, ndom - 1, answer, 0)
    lax.fori_loop(0, ndom - 1, answered, 0)


def body(
    features, send_rows, neighbours, w_self1, w_neigh1, w_self2, w_neigh2, queries, owners, slate
):
    ndom, nrep = lax.axis_size("dom"), lax.axis_size("rep")
    nx, nz = 4, 8
    nodes, width = features.shape
    fan = neighbours.shape[1]
    per_pair = send_rows.shape[1]
    chunk = nodes // nrep
    full = width * nrep
    sessions, topq, nitems = slate.shape
    capacity = min(sessions, 2 * sessions * topq // ndom)
    entries, nslots = sessions * topq, ndom * capacity
    count = capacity * nitems
    half = count // LANE
    qrows = capacity

    send_idx = send_rows.reshape(-1)
    neigh_idx = neighbours.T.reshape(-1)

    owner_of = owners.T.reshape(entries)
    named = owner_of[:, None] == jnp.arange(ndom, dtype=jnp.int32)[None, :]
    order = jnp.arange(entries, dtype=jnp.int32)
    earlier = (order[:, None] > order[None, :]).astype(BF16)
    before = jnp.dot(earlier, named.astype(BF16), preferred_element_type=F32)
    position = jnp.sum(jnp.where(named, before, 0.0), axis=1).astype(jnp.int32)
    slot_index = owner_of * capacity + position
    place = (jnp.arange(nslots, dtype=jnp.int32)[:, None] == slot_index[None, :]).astype(BF16)
    slot_queries = jnp.dot(place, jnp.tile(queries, (topq, 1)), preferred_element_type=F32)
    asked = slot_queries.astype(BF16)
    lists = slate.transpose(1, 0, 2).reshape(entries, nitems)
    digits = jnp.concatenate([lists // 64, lists % 64], axis=1).astype(BF16)
    slot_digits = jnp.dot(place, digits, preferred_element_type=F32).astype(jnp.int32)
    slot_lists = slot_digits[:, :nitems] * 64 + slot_digits[:, nitems:]
    slot_lists = slot_lists.reshape(ndom, capacity, nitems).transpose(0, 2, 1)
    slot_lists = slot_lists.reshape(ndom, half, LANE)

    dma = pltpu.SemaphoreType.DMA
    shape = jax.ShapeDtypeStruct
    whole = pl.BlockSpec(memory_space=VMEM)
    peers, others = (ndom - 1,), (nrep - 1,)
    args = [neigh_idx, send_idx, features, w_self1, w_neigh1, w_self2, w_neigh2, asked, slot_lists]
    per_layer = [dma(others), dma(others), dma((TILES, nrep - 1)), dma((TILES, nrep - 1)), dma((1 + TILES,))]
    node_embed, fetched = pl.pallas_call(
        functools.partial(kernel, nrep, ndom, nx, nz, fan, nitems),
        out_shape=[shape((nodes, width), BF16), shape((ndom, half, LANE), F32)],
        in_specs=[pl.BlockSpec(memory_space=pltpu.SMEM)] * 2 + [whole] * (len(args) - 2),
        out_specs=[whole, whole],
        scratch_shapes=[
            VMEM((nodes + ndom * per_pair, width), F32),
            VMEM((chunk, width), F32),
            VMEM((per_pair, width), F32),
            VMEM((count, width), F32),
            VMEM((ndom * per_pair, width), BF16),
            VMEM((ndom * per_pair, width), BF16),
            VMEM((ndom * per_pair, width), BF16),
            VMEM((nrep, chunk, width), BF16),
            VMEM((nrep, chunk, width), BF16),
            VMEM((chunk, full), BF16),
            VMEM((chunk, full), BF16),
            VMEM((chunk, full), BF16),
            VMEM((chunk, full), BF16),
            VMEM((chunk, full), BF16),
            VMEM((nodes, width), BF16),
            VMEM((2 * full, full), BF16),
            VMEM((2 * full, full), BF16),
            VMEM((ndom * qrows, LANE), BF16),
            VMEM((ndom, half, LANE), jnp.int32),
            pltpu.SMEM((ndom, half, LANE), jnp.int32),
            VMEM((nrep, ndom, half, LANE), F32),
            VMEM((ndom, half, LANE), F32),
        ]
        + [dma(peers)] * 10
        + [dma(others)] * 2
        + [dma((4, nrep - 1))] * 2
        + [dma(others)] * 2
        + per_layer
        + per_layer
        + [dma((9,))],
        compiler_params=pltpu.CompilerParams(
            collective_id=1, has_side_effects=True, vmem_limit_bytes=56 * 1024 * 1024
        ),
        name="graph_and_scores",
    )(*args)
    fetched = fetched.reshape(ndom, nitems, capacity).transpose(0, 2, 1).reshape(nslots, nitems)
    scores = fetched[slot_index].reshape(topq, sessions, nitems)
    return (node_embed, scores.transpose(1, 0, 2).reshape(sessions, topq * nitems))


def solution(mesh):
    placed = (
        P("dom", "rep"),
        P("dom", None),
        P("dom", None),
        P(None, "rep"),
        P(None, "rep"),
        P(None, "rep"),
        P(None, "rep"),
        P("dom", "rep"),
        P("dom", None),
        P("dom", None, None),
    )
    return jax.shard_map(
        body,
        mesh=mesh,
        in_specs=placed,
        out_specs=(P("dom", "rep"), P("dom", None)),
        check_vma=False,
    )
```

```python
import functools

import jax
import jax.numpy as jnp
from jax import lax
from jax.experimental import pallas as pl
from jax.experimental.pallas import tpu as pltpu
from jax.sharding import PartitionSpec as P

MESH = pl.DeviceIdType.MESH
VMEM = pltpu.VMEM
F32 = jnp.float32
BF16 = jnp.bfloat16
LANE = 128
EPS = 1e-06
TILES = 4


def columns_of(which):
    return pl.ds(pl.multiple_of(which * LANE, LANE), LANE)


def rows_of(which, count):
    return pl.ds(pl.multiple_of(which * count, count), count)


class Ring:
    def __init__(self, ndom, nx, nz):
        self.ndom, self.nx, self.nz = ndom, nx, nz
        me = lax.axis_index("dom")
        self.me = me
        self.core = lax.rem(me, 2)
        self.z = lax.rem(lax.div(me, 2), nz)
        self.x = lax.div(me, 2 * nz)

    def offset(self, n):
        nz, nx = self.nz, self.nx
        i = lax.rem(n, nz)
        dz = nz // 2 + (1 - 2 * lax.rem(i, 2)) * lax.div(i + 1, 2)
        turn = lax.div(n, nz)
        return lax.rem(lax.div(turn, 2) + 1, nx), dz, 1 - lax.rem(turn, 2)

    def target(self, n):
        dx, dz, dc = self.offset(n)
        x = lax.rem(self.x + dx, self.nx)
        z = lax.rem(self.z + dz, self.nz)
        return (x * self.nz + z) * 2 + lax.rem(self.core + dc, 2)

    def source(self, n):
        dx, dz, dc = self.offset(n)
        x = lax.rem(self.x - dx + self.nx, self.nx)
        z = lax.rem(self.z - dz + self.nz, self.nz)
        return (x * self.nz + z) * 2 + lax.rem(self.core + dc, 2)


def to_dom(src, dst, send, recv, target):
    return pltpu.make_async_remote_copy(
        src_ref=src, dst_ref=dst, send_sem=send, recv_sem=recv,
        device_id={"dom": target}, device_id_type=MESH,
    )


def to_rep(src, dst, send, recv, target):
    return pltpu.make_async_remote_copy(
        src_ref=src, dst_ref=dst, send_sem=send, recv_sem=recv,
        device_id={"rep": target}, device_id_type=MESH,
    )


def pick_rows(index_of, table, stage, unroll):
    def some(block, carry):
        base = block * unroll
        for u in range(unroll):
            stage[pl.ds(base + u, 1), :] = table[pl.ds(index_of(base, u), 1), :]
        return carry

    lax.fori_loop(0, stage.shape[0] // unroll, some, 0)


def sum_rows(index_ref, start, table, stage, nodes, fan, unroll):
    def some(block, carry):
        base = block * unroll
        for u in range(unroll):
            terms = [
                table[pl.ds(index_ref[k * nodes + start + base + u], 1), :] for k in range(fan)
            ]
            while len(terms) > 1:
                pairs = [terms[i] + terms[i + 1] for i in range(0, len(terms) - 1, 2)]
                terms = pairs + terms[len(pairs) * 2 :]
            stage[pl.ds(base + u, 1), :] = terms[0]
        return carry

    lax.fori_loop(0, stage.shape[0] // unroll, some, 0)


def start_boundary(ring, send_idx, table, nodes, pick, outgoing, landing, send, recv):
    count = pick.shape[0]

    def one(n, carry):
        to = ring.target(n)
        pick_rows(lambda base, u: send_idx[to * count + base + u], table, pick, 32)
        outgoing[rows_of(to, count), :] = pick[...].astype(BF16)
        to_dom(
            outgoing.at[rows_of(to, count), :],
            landing.at[rows_of(ring.me, count), :],
            send.at[n],
            recv.at[n],
            to,
        ).start()
        return carry

    lax.fori_loop(0, ring.ndom - 1, one, 0)
    me = ring.me
    pick_rows(lambda base, u: send_idx[me * count + base + u], table, pick, 32)
    table[pl.ds(pl.multiple_of(nodes + me * count, 64), count), :] = pick[...]


def finish_boundary(ring, table, nodes, count, outgoing, landing, send, recv):
    def one(n, carry):
        to, source = ring.target(n), ring.source(n)
        copy = to_dom(
            outgoing.at[rows_of(to, count), :],
            landing.at[rows_of(source, count), :],
            send.at[n],
            recv.at[n],
            to,
        )
        copy.wait_recv()
        table[pl.ds(pl.multiple_of(nodes + source * count, 64), count), :] = landing[
            rows_of(source, count), :
        ].astype(F32)
        copy.wait_send()
        return carry

    lax.fori_loop(0, ring.ndom - 1, one, 0)


def layer(
    active, me, nrep, fan, neigh_idx, nodes, table, stage, before_product,
    self_rows, weights, chunks, agg_rows, hid_rows, hid_cols, send, recv, hsend, hrecv, local,
):
    chunk = nodes // nrep
    width = self_rows.shape[1]
    tile = chunk // TILES

    def there(t):
        return agg_rows.at[pl.ds(t * tile, tile), columns_of(me)]

    def sum_copy(t, step):
        to = lax.rem(me + 1 + step, nrep)
        return to_rep(chunks.at[t, step], there(t), send.at[t, step], recv.at[t, step], to)

    def own_sum_copy(t):
        return pltpu.make_async_copy(chunks.at[t, nrep - 1], there(t), local.at[0, t])

    def sums(t):
        def summed(step):
            to = lax.rem(me + 1 + step, nrep)
            sum_rows(neigh_idx, to * chunk + t * tile, table, stage, nodes, fan, 16)
            chunks[t, step] = (stage[...] / fan).astype(BF16)

        def one(step, carry):
            summed(step)
            sum_copy(t, step).start()
            return carry

        lax.fori_loop(0, nrep - 1, one, 0)
        summed(nrep - 1)
        own_sum_copy(t).start()

    back = []

    def product(t):
        for step in range(nrep - 1):
            sum_copy(t, step).wait()
        own_sum_copy(t).wait()
        rows = pl.ds(t * tile, tile)
        z = jnp.dot(self_rows[rows, :], weights[pl.ds(0, width), :], preferred_element_type=F32)
        z = z + jnp.dot(
            agg_rows[rows, :], weights[pl.ds(width, width), :], preferred_element_type=F32
        )
        if active:
            z = jnp.maximum(z, 0.0)
        mean = jnp.sum(z * z, axis=1, keepdims=True) / width
        hid_rows[rows, :] = (z * lax.rsqrt(mean + EPS)).astype(BF16)
        landing = hid_cols.at[pl.ds(pl.multiple_of(me * chunk + t * tile, tile), tile), :]
        for step in range(nrep - 1):
            to = lax.rem(me + 1 + step, nrep)
            copy = to_rep(
                hid_rows.at[rows, columns_of(to)], landing, hsend.at[t, step], hrecv.at[t, step], to
            )
            copy.start()
            back.append(copy)
        copy = pltpu.make_async_copy(hid_rows.at[rows, columns_of(me)], landing, local.at[1, t])
        copy.start()
        back.append(copy)

    sums(0)
    for copy in before_product:
        copy.wait()
    for t in range(1, TILES):
        sums(t)
        product(t - 1)
    product(TILES - 1)
    for copy in back:
        copy.wait()
    table[pl.ds(0, nodes), :] = hid_cols[...].astype(F32)


def kernel(
    nrep, ndom, nx, nz, fan, nitems,
    neigh_idx, send_idx, own, wself1, wneigh1, wself2, wneigh2, asked, lists,
    embed, fetched,
    table, stage, pick, found, outgoing, landing1, landing2, chunks1, chunks2, agg1, agg2,
    x_rows, h_rows, e_rows, h_cols, weights1, weights2, got, got_lists, items, partial, total,
    bsend1, brecv1, bsend2, brecv2, qsend, qrecv, isend, irecv, fsend, frecv, xsend, xrecv, wsend, wrecv,
    psend, precv, asend1, arecv1, hsend1, hrecv1, local1, asend2, arecv2, hsend2, hrecv2, local2,
    local,
):
    ring = Ring(ndom, nx, nz)
    me = lax.axis_index("rep")
    nodes = own.shape[0]
    chunk = nodes // nrep
    full = h_rows.shape[1]

    barrier = pltpu.get_barrier_semaphore()

    def greet(n, carry):
        pl.semaphore_signal(barrier, inc=1, device_id={"dom": ring.target(n)}, device_id_type=MESH)
        return carry

    lax.fori_loop(0, ndom - 1, greet, 0)
    for step in range(1, nrep):
        pl.semaphore_signal(
            barrier, inc=1, device_id={"rep": lax.rem(me + step, nrep)}, device_id_type=MESH
        )
    table[pl.ds(0, nodes), :] = own[...].astype(F32)
    pl.semaphore_wait(barrier, ndom - 1 + nrep - 1)

    early = []
    blocks = (
        (wself1, weights1, 0), (wneigh1, weights1, full),
        (wself2, weights2, 0), (wneigh2, weights2, full),
    )
    for step in range(nrep - 1):
        to = lax.rem(me + 1 + step, nrep)
        early.append(
            to_rep(own.at[rows_of(to, chunk), :], x_rows.at[:, columns_of(me)],
                   xsend.at[step], xrecv.at[step], to)
        )
        for b, (part, whole, at) in enumerate(blocks):
            early.append(
                to_rep(part, whole.at[pl.ds(at, full), columns_of(me)],
                       wsend.at[b, step], wrecv.at[b, step], to)
            )
    early.append(
        pltpu.make_async_copy(own.at[rows_of(me, chunk), :], x_rows.at[:, columns_of(me)], local.at[0])
    )
    for b, (part, whole, at) in enumerate(blocks):
        early.append(
            pltpu.make_async_copy(part, whole.at[pl.ds(at, full), columns_of(me)], local.at[1 + b])
        )
    for copy in early:
        copy.start()

    count = pick.shape[0]
    start_boundary(ring, send_idx, table, nodes, pick, outgoing, landing1, bsend1, brecv1)
    finish_boundary(ring, table, nodes, count, outgoing, landing1, bsend1, brecv1)

    qrows = got.shape[0] // ndom
    own_asked = [
        pltpu.make_async_copy(
            asked.at[rows_of(ring.me, qrows), :], got.at[rows_of(ring.me, qrows), :],
            local.at[1 + len(blocks)],
        ),
        pltpu.make_async_copy(
            lists.at[ring.me], got_lists.at[ring.me], local.at[2 + len(blocks)]
        ),
    ]
    for copy in own_asked:
        copy.start()

    def query_copies(n, origin):
        to = ring.target(n)
        return (
            to_dom(asked.at[rows_of(to, qrows), :], got.at[rows_of(origin, qrows), :],
                   qsend.at[n], qrecv.at[n], to),
            to_dom(lists.at[to], got_lists.at[origin], isend.at[n], irecv.at[n], to),
        )

    def ask(n, carry):
        for copy in query_copies(n, ring.me):
            copy.start()
        return carry

    lax.fori_loop(0, ndom - 1, ask, 0)
    layer(
        True, me, nrep, fan, neigh_idx, nodes, table, stage, early, x_rows, weights1,
        chunks1, agg1, h_rows, h_cols, asend1, arecv1, hsend1, hrecv1, local1,
    )
    start_boundary(ring, send_idx, table, nodes, pick, outgoing, landing2, bsend2, brecv2)

    def asked_by(n, carry):
        for copy in query_copies(n, ring.source(n)):
            copy.wait()
        return carry

    lax.fori_loop(0, ndom - 1, asked_by, 0)
    for copy in own_asked:
        copy.wait()
    into = pltpu.make_async_copy(got_lists, items, local.at[3 + len(blocks)])
    into.start()
    into.wait()
    finish_boundary(ring, table, nodes, count, outgoing, landing2, bsend2, brecv2)
    layer(
        False, me, nrep, fan, neigh_idx, nodes, table, stage, [], h_rows, weights2,
        chunks2, agg2, e_rows, embed, asend2, arecv2, hsend2, hrecv2, local2,
    )

    slots = qrows
    half = got_lists.shape[1]
    wide = half * LANE
    owns = lax.broadcasted_iota(jnp.int32, (slots, wide), 0)
    slot = lax.rem(lax.broadcasted_iota(jnp.int32, (slots, wide), 1), slots)

    def find(p, carry):
        base = pl.multiple_of(p * wide, wide)
        for h in range(half):
            for i in range(LANE):
                found[pl.ds(base + (h * LANE + i), 1), :] = table[pl.ds(items[p, h, i], 1), :]
        return carry

    lax.fori_loop(0, ndom, find, 0)
    together = 4

    def score(block, carry):
        for u in range(together):
            p = block * together + u
            products = lax.dot_general(
                got[rows_of(p, slots), :],
                found[rows_of(p, wide), :].astype(BF16),
                (((1,), (1,)), ((), ())),
                preferred_element_type=F32,
            )
            kept = jnp.sum(jnp.where(owns == slot, products, 0.0), axis=0, keepdims=True)
            for h in range(half):
                partial[me, p, pl.ds(h, 1), :] = kept[:, h * LANE : (h + 1) * LANE]
        return carry

    lax.fori_loop(0, ndom // together, score, 0)
    copies = []
    for step in range(nrep - 1):
        copy = to_rep(partial.at[me], partial.at[me], psend.at[step], precv.at[step],
                      lax.rem(me + 1 + step, nrep))
        copy.start()
        copies.append(copy)
    for copy in copies:
        copy.wait()
    added = partial[0]
    for other in range(1, nrep):
        added = added + partial[other]
    total[...] = added
    fetched[ring.me] = total[ring.me]

    def answer(n, carry):
        to = ring.target(n)
        to_dom(total.at[to], fetched.at[ring.me], fsend.at[n], frecv.at[n], to).start()
        return carry

    def answered(n, carry):
        to, source = ring.target(n), ring.source(n)
        to_dom(total.at[to], fetched.at[source], fsend.at[n], frecv.at[n], to).wait()
        return carry

    lax.fori_loop(0, ndom - 1, answer, 0)
    lax.fori_loop(0, ndom - 1, answered, 0)


def body(
    features, send_rows, neighbours, w_self1, w_neigh1, w_self2, w_neigh2, queries, owners, slate
):
    ndom, nrep = lax.axis_size("dom"), lax.axis_size("rep")
    nx, nz = 4, 8
    nodes, width = features.shape
    fan = neighbours.shape[1]
    per_pair = send_rows.shape[1]
    chunk = nodes // nrep
    full = width * nrep
    sessions, topq, nitems = slate.shape
    capacity = min(sessions, 2 * sessions * topq // ndom)
    entries, nslots = sessions * topq, ndom * capacity
    count = capacity * nitems
    half = count // LANE
    qrows = capacity

    send_idx = send_rows.reshape(-1)
    neigh_idx = neighbours.T.reshape(-1)

    owner_of = owners.T.reshape(entries)
    named = owner_of[:, None] == jnp.arange(ndom, dtype=jnp.int32)[None, :]
    order = jnp.arange(entries, dtype=jnp.int32)
    earlier = (order[:, None] > order[None, :]).astype(BF16)
    before = jnp.dot(earlier, named.astype(BF16), preferred_element_type=F32)
    position = jnp.sum(jnp.where(named, before, 0.0), axis=1).astype(jnp.int32)
    slot_index = owner_of * capacity + position
    place = (jnp.arange(nslots, dtype=jnp.int32)[:, None] == slot_index[None, :]).astype(BF16)
    slot_queries = jnp.dot(place, jnp.tile(queries, (topq, 1)), preferred_element_type=F32)
    asked = slot_queries.astype(BF16)
    lists = slate.transpose(1, 0, 2).reshape(entries, nitems)
    digits = jnp.concatenate([lists // 64, lists % 64], axis=1).astype(BF16)
    slot_digits = jnp.dot(place, digits, preferred_element_type=F32).astype(jnp.int32)
    slot_lists = slot_digits[:, :nitems] * 64 + slot_digits[:, nitems:]
    slot_lists = slot_lists.reshape(ndom, capacity, nitems).transpose(0, 2, 1)
    slot_lists = slot_lists.reshape(ndom, half, LANE)

    dma = pltpu.SemaphoreType.DMA
    shape = jax.ShapeDtypeStruct
    whole = pl.BlockSpec(memory_space=VMEM)
    peers, others = (ndom - 1,), (nrep - 1,)
    args = [neigh_idx, send_idx, features, w_self1, w_neigh1, w_self2, w_neigh2, asked, slot_lists]
    per_layer = [dma((TILES, nrep - 1))] * 4 + [dma((2, TILES))]
    node_embed, fetched = pl.pallas_call(
        functools.partial(kernel, nrep, ndom, nx, nz, fan, nitems),
        out_shape=[shape((nodes, width), BF16), shape((ndom, half, LANE), F32)],
        in_specs=[pl.BlockSpec(memory_space=pltpu.SMEM)] * 2 + [whole] * (len(args) - 2),
        out_specs=[whole, whole],
        scratch_shapes=[
            VMEM((nodes + ndom * per_pair, width), F32),
            VMEM((chunk // TILES, width), F32),
            VMEM((per_pair, width), F32),
            VMEM((ndom * count, width), F32),
            VMEM((ndom * per_pair, width), BF16),
            VMEM((ndom * per_pair, width), BF16),
            VMEM((ndom * per_pair, width), BF16),
            VMEM((TILES, nrep, chunk // TILES, width), BF16),
            VMEM((TILES, nrep, chunk // TILES, width), BF16),
            VMEM((chunk, full), BF16),
            VMEM((chunk, full), BF16),
            VMEM((chunk, full), BF16),
            VMEM((chunk, full), BF16),
            VMEM((chunk, full), BF16),
            VMEM((nodes, width), BF16),
            VMEM((2 * full, full), BF16),
            VMEM((2 * full, full), BF16),
            VMEM((ndom * qrows, LANE), BF16),
            VMEM((ndom, half, LANE), jnp.int32),
            pltpu.SMEM((ndom, half, LANE), jnp.int32),
            VMEM((nrep, ndom, half, LANE), F32),
            VMEM((ndom, half, LANE), F32),
        ]
        + [dma(peers)] * 10
        + [dma(others)] * 2
        + [dma((4, nrep - 1))] * 2
        + [dma(others)] * 2
        + per_layer
        + per_layer
        + [dma((9,))],
        compiler_params=pltpu.CompilerParams(
            collective_id=1, has_side_effects=True, vmem_limit_bytes=56 * 1024 * 1024
        ),
        name="graph_and_scores",
    )(*args)
    fetched = fetched.reshape(ndom, nitems, capacity).transpose(0, 2, 1).reshape(nslots, nitems)
    scores = fetched[slot_index].reshape(topq, sessions, nitems)
    return (node_embed, scores.transpose(1, 0, 2).reshape(sessions, topq * nitems))


def solution(mesh):
    placed = (
        P("dom", "rep"),
        P("dom", None),
        P("dom", None),
        P(None, "rep"),
        P(None, "rep"),
        P(None, "rep"),
        P(None, "rep"),
        P("dom", "rep"),
        P("dom", None),
        P("dom", None, None),
    )
    return jax.shard_map(
        body,
        mesh=mesh,
        in_specs=placed,
        out_specs=(P("dom", "rep"), P("dom", None)),
        check_vma=False,
    )
```

```python
import functools

import jax
import jax.numpy as jnp
from jax import lax
from jax.experimental import pallas as pl
from jax.experimental.pallas import tpu as pltpu
from jax.sharding import PartitionSpec as P

MESH = pl.DeviceIdType.MESH
VMEM = pltpu.VMEM
F32 = jnp.float32
BF16 = jnp.bfloat16
LANE = 128
EPS = 1e-06
TILES = 4


def columns_of(which):
    return pl.ds(pl.multiple_of(which * LANE, LANE), LANE)


def rows_of(which, count):
    return pl.ds(pl.multiple_of(which * count, count), count)


class Ring:
    def __init__(self, ndom, nx, nz):
        self.ndom, self.nx, self.nz = ndom, nx, nz
        me = lax.axis_index("dom")
        self.me = me
        self.core = lax.rem(me, 2)
        self.z = lax.rem(lax.div(me, 2), nz)
        self.x = lax.div(me, 2 * nz)

    def offset(self, n):
        nz, nx = self.nz, self.nx
        i = lax.rem(n, nz)
        dz = nz // 2 + (1 - 2 * lax.rem(i, 2)) * lax.div(i + 1, 2)
        turn = lax.div(n, nz)
        return lax.rem(lax.div(turn, 2) + 1, nx), dz, 1 - lax.rem(turn, 2)

    def target(self, n):
        dx, dz, dc = self.offset(n)
        x = lax.rem(self.x + dx, self.nx)
        z = lax.rem(self.z + dz, self.nz)
        return (x * self.nz + z) * 2 + lax.rem(self.core + dc, 2)

    def source(self, n):
        dx, dz, dc = self.offset(n)
        x = lax.rem(self.x - dx + self.nx, self.nx)
        z = lax.rem(self.z - dz + self.nz, self.nz)
        return (x * self.nz + z) * 2 + lax.rem(self.core + dc, 2)


def to_dom(src, dst, send, recv, target):
    return pltpu.make_async_remote_copy(
        src_ref=src, dst_ref=dst, send_sem=send, recv_sem=recv,
        device_id={"dom": target}, device_id_type=MESH,
    )


def to_rep(src, dst, send, recv, target):
    return pltpu.make_async_remote_copy(
        src_ref=src, dst_ref=dst, send_sem=send, recv_sem=recv,
        device_id={"rep": target}, device_id_type=MESH,
    )


def pick_rows(index_of, table, stage, unroll):
    def some(block, carry):
        base = block * unroll
        for u in range(unroll):
            stage[pl.ds(base + u, 1), :] = table[pl.ds(index_of(base, u), 1), :]
        return carry

    lax.fori_loop(0, stage.shape[0] // unroll, some, 0)


def sum_rows(index_ref, start, table, stage, nodes, fan, unroll):
    span = nodes - unroll + 1

    def some(block, carry):
        base = block * unroll
        for u in range(unroll):
            terms = [
                table[pl.ds(index_ref.at[pl.ds(k * nodes + u, span)][start + base], 1), :]
                for k in range(fan)
            ]
            while len(terms) > 1:
                pairs = [terms[i] + terms[i + 1] for i in range(0, len(terms) - 1, 2)]
                terms = pairs + terms[len(pairs) * 2 :]
            stage[pl.ds(base + u, 1), :] = terms[0]
        return carry

    lax.fori_loop(0, stage.shape[0] // unroll, some, 0)


def start_boundary(ring, send_idx, table, nodes, pick, outgoing, landing, send, recv):
    count = pick.shape[0]

    def one(n, carry):
        to = ring.target(n)
        pick_rows(lambda base, u: send_idx[to * count + base + u], table, pick, 32)
        outgoing[rows_of(to, count), :] = pick[...].astype(BF16)
        to_dom(
            outgoing.at[rows_of(to, count), :],
            landing.at[rows_of(ring.me, count), :],
            send.at[n],
            recv.at[n],
            to,
        ).start()
        return carry

    lax.fori_loop(0, ring.ndom - 1, one, 0)
    me = ring.me
    pick_rows(lambda base, u: send_idx[me * count + base + u], table, pick, 32)
    table[pl.ds(pl.multiple_of(nodes + me * count, 64), count), :] = pick[...]


def finish_boundary(ring, table, nodes, count, outgoing, landing, send, recv):
    def one(n, carry):
        to, source = ring.target(n), ring.source(n)
        copy = to_dom(
            outgoing.at[rows_of(to, count), :],
            landing.at[rows_of(source, count), :],
            send.at[n],
            recv.at[n],
            to,
        )
        copy.wait_recv()
        table[pl.ds(pl.multiple_of(nodes + source * count, 64), count), :] = landing[
            rows_of(source, count), :
        ].astype(F32)
        copy.wait_send()
        return carry

    lax.fori_loop(0, ring.ndom - 1, one, 0)


def layer(
    active, me, nrep, fan, neigh_idx, nodes, table, stage, before_product,
    self_rows, weights, chunks, agg_rows, hid_rows, hid_cols, send, recv, hsend, hrecv, local,
):
    chunk = nodes // nrep
    width = self_rows.shape[1]
    tile = chunk // TILES

    def there(t):
        return agg_rows.at[pl.ds(t * tile, tile), columns_of(me)]

    def sum_copy(t, step):
        to = lax.rem(me + 1 + step, nrep)
        return to_rep(chunks.at[t, step], there(t), send.at[t, step], recv.at[t, step], to)

    def own_sum_copy(t):
        return pltpu.make_async_copy(chunks.at[t, nrep - 1], there(t), local.at[0, t])

    def sums(t):
        def summed(step):
            to = lax.rem(me + 1 + step, nrep)
            sum_rows(neigh_idx, to * chunk + t * tile, table, stage, nodes, fan, 32)
            chunks[t, step] = (stage[...] / fan).astype(BF16)

        def one(step, carry):
            summed(step)
            sum_copy(t, step).start()
            return carry

        lax.fori_loop(0, nrep - 1, one, 0)
        summed(nrep - 1)
        own_sum_copy(t).start()

    back = []

    def product(t):
        for step in range(nrep - 1):
            sum_copy(t, step).wait()
        own_sum_copy(t).wait()
        rows = pl.ds(t * tile, tile)
        z = jnp.dot(self_rows[rows, :], weights[pl.ds(0, width), :], preferred_element_type=F32)
        z = z + jnp.dot(
            agg_rows[rows, :], weights[pl.ds(width, width), :], preferred_element_type=F32
        )
        if active:
            z = jnp.maximum(z, 0.0)
        mean = jnp.sum(z * z, axis=1, keepdims=True) / width
        hid_rows[rows, :] = (z * lax.rsqrt(mean + EPS)).astype(BF16)
        landing = hid_cols.at[pl.ds(pl.multiple_of(me * chunk + t * tile, tile), tile), :]
        for step in range(nrep - 1):
            to = lax.rem(me + 1 + step, nrep)
            copy = to_rep(
                hid_rows.at[rows, columns_of(to)], landing, hsend.at[t, step], hrecv.at[t, step], to
            )
            copy.start()
            back.append(copy)
        copy = pltpu.make_async_copy(hid_rows.at[rows, columns_of(me)], landing, local.at[1, t])
        copy.start()
        back.append(copy)

    sums(0)
    for copy in before_product:
        copy.wait()
    for t in range(1, TILES):
        sums(t)
        product(t - 1)
    product(TILES - 1)
    for copy in back:
        copy.wait()
    table[pl.ds(0, nodes), :] = hid_cols[...].astype(F32)


def kernel(
    nrep, ndom, nx, nz, fan, nitems,
    neigh_idx, send_idx, own, wself1, wneigh1, wself2, wneigh2, queries, lists, slot_of,
    embed, scores,
    table, stage, pick, found, outgoing, landing1, landing2, chunks1, chunks2, agg1, agg2,
    x_rows, h_rows, e_rows, h_cols, weights1, weights2, got, got_lists, items, partial, total, fetched, asked,
    bsend1, brecv1, bsend2, brecv2, qsend, qrecv, isend, irecv, fsend, frecv, xsend, xrecv, wsend, wrecv,
    psend, precv, asend1, arecv1, hsend1, hrecv1, local1, asend2, arecv2, hsend2, hrecv2, local2,
    local,
):
    ring = Ring(ndom, nx, nz)
    me = lax.axis_index("rep")
    nodes = own.shape[0]
    chunk = nodes // nrep
    full = h_rows.shape[1]

    barrier = pltpu.get_barrier_semaphore()

    def greet(n, carry):
        pl.semaphore_signal(barrier, inc=1, device_id={"dom": ring.target(n)}, device_id_type=MESH)
        return carry

    lax.fori_loop(0, ndom - 1, greet, 0)
    for step in range(1, nrep):
        pl.semaphore_signal(
            barrier, inc=1, device_id={"rep": lax.rem(me + step, nrep)}, device_id_type=MESH
        )
    table[pl.ds(0, nodes), :] = own[...].astype(F32)
    pl.semaphore_wait(barrier, ndom - 1 + nrep - 1)

    early = []
    blocks = (
        (wself1, weights1, 0), (wneigh1, weights1, full),
        (wself2, weights2, 0), (wneigh2, weights2, full),
    )
    for step in range(nrep - 1):
        to = lax.rem(me + 1 + step, nrep)
        early.append(
            to_rep(own.at[rows_of(to, chunk), :], x_rows.at[:, columns_of(me)],
                   xsend.at[step], xrecv.at[step], to)
        )
        for b, (part, whole, at) in enumerate(blocks):
            early.append(
                to_rep(part, whole.at[pl.ds(at, full), columns_of(me)],
                       wsend.at[b, step], wrecv.at[b, step], to)
            )
    early.append(
        pltpu.make_async_copy(own.at[rows_of(me, chunk), :], x_rows.at[:, columns_of(me)], local.at[0])
    )
    for b, (part, whole, at) in enumerate(blocks):
        early.append(
            pltpu.make_async_copy(part, whole.at[pl.ds(at, full), columns_of(me)], local.at[1 + b])
        )
    for copy in early:
        copy.start()

    count = pick.shape[0]
    start_boundary(ring, send_idx, table, nodes, pick, outgoing, landing1, bsend1, brecv1)
    sessions = queries.shape[0]
    topq = slot_of.shape[0]

    def fill(block, carry):
        slot = lax.broadcasted_iota(jnp.int32, (sessions, sessions), 0) + block * sessions
        rows = jnp.zeros((sessions, LANE), F32)
        for t in range(topq):
            place = jnp.where(slot_of[t : t + 1, :] == slot, 1.0, 0.0).astype(BF16)
            rows = rows + jnp.dot(place, queries[...], preferred_element_type=F32)
        asked[rows_of(block, sessions), :] = rows.astype(BF16)
        return carry

    lax.fori_loop(0, asked.shape[0] // sessions, fill, 0)
    finish_boundary(ring, table, nodes, count, outgoing, landing1, bsend1, brecv1)

    qrows = got.shape[0] // ndom
    own_asked = [
        pltpu.make_async_copy(
            asked.at[rows_of(ring.me, qrows), :], got.at[rows_of(ring.me, qrows), :],
            local.at[1 + len(blocks)],
        ),
        pltpu.make_async_copy(
            lists.at[ring.me], got_lists.at[ring.me], local.at[2 + len(blocks)]
        ),
    ]
    for copy in own_asked:
        copy.start()

    def query_copies(n, origin):
        to = ring.target(n)
        return (
            to_dom(asked.at[rows_of(to, qrows), :], got.at[rows_of(origin, qrows), :],
                   qsend.at[n], qrecv.at[n], to),
            to_dom(lists.at[to], got_lists.at[origin], isend.at[n], irecv.at[n], to),
        )

    def ask(n, carry):
        for copy in query_copies(n, ring.me):
            copy.start()
        return carry

    lax.fori_loop(0, ndom - 1, ask, 0)
    layer(
        True, me, nrep, fan, neigh_idx, nodes, table, stage, early, x_rows, weights1,
        chunks1, agg1, h_rows, h_cols, asend1, arecv1, hsend1, hrecv1, local1,
    )
    start_boundary(ring, send_idx, table, nodes, pick, outgoing, landing2, bsend2, brecv2)

    def asked_by(n, carry):
        for copy in query_copies(n, ring.source(n)):
            copy.wait()
        return carry

    lax.fori_loop(0, ndom - 1, asked_by, 0)
    for copy in own_asked:
        copy.wait()
    into = pltpu.make_async_copy(got_lists, items, local.at[3 + len(blocks)])
    into.start()
    into.wait()
    finish_boundary(ring, table, nodes, count, outgoing, landing2, bsend2, brecv2)
    layer(
        False, me, nrep, fan, neigh_idx, nodes, table, stage, [], h_rows, weights2,
        chunks2, agg2, e_rows, embed, asend2, arecv2, hsend2, hrecv2, local2,
    )

    slots = qrows
    half = got_lists.shape[1]
    wide = half * LANE
    owns = lax.broadcasted_iota(jnp.int32, (slots, wide), 0)
    slot = lax.rem(lax.broadcasted_iota(jnp.int32, (slots, wide), 1), slots)

    def find(p, carry):
        base = pl.multiple_of(p * wide, wide)
        for h in range(half):
            for i in range(LANE):
                item = items.at[:, pl.ds(h, 1), pl.ds(i, 1)][p, 0, 0]
                found[pl.ds(base + (h * LANE + i), 1), :] = table[pl.ds(item, 1), :]
        return carry

    lax.fori_loop(0, ndom, find, 0)
    together = 4

    def score(block, carry):
        for u in range(together):
            p = block * together + u
            products = lax.dot_general(
                got[rows_of(p, slots), :],
                found[rows_of(p, wide), :].astype(BF16),
                (((1,), (1,)), ((), ())),
                preferred_element_type=F32,
            )
            kept = jnp.sum(jnp.where(owns == slot, products, 0.0), axis=0, keepdims=True)
            for h in range(half):
                partial[me, p, pl.ds(h, 1), :] = kept[:, h * LANE : (h + 1) * LANE]
        return carry

    lax.fori_loop(0, ndom // together, score, 0)
    copies = []
    for step in range(nrep - 1):
        copy = to_rep(partial.at[me], partial.at[me], psend.at[step], precv.at[step],
                      lax.rem(me + 1 + step, nrep))
        copy.start()
        copies.append(copy)
    for copy in copies:
        copy.wait()
    added = partial[0]
    for other in range(1, nrep):
        added = added + partial[other]
    total[...] = added
    fetched[ring.me] = total[ring.me]

    def answer(n, carry):
        to = ring.target(n)
        to_dom(total.at[to], fetched.at[ring.me], fsend.at[n], frecv.at[n], to).start()
        return carry

    def answered(n, carry):
        to, source = ring.target(n), ring.source(n)
        to_dom(total.at[to], fetched.at[source], fsend.at[n], frecv.at[n], to).wait()
        return carry

    lax.fori_loop(0, ndom - 1, answer, 0)
    lax.fori_loop(0, ndom - 1, answered, 0)

    parts = []
    for h in range(half):
        rest, split = fetched[:, h, :], []
        for _ in range(3):
            split.append(rest.astype(BF16))
            rest = rest - split[-1].astype(F32)
        parts.append(split)
    partition = lax.broadcasted_iota(jnp.int32, (ndom, sessions), 0)
    position = lax.rem(lax.broadcasted_iota(jnp.int32, (LANE, sessions), 0), slots)
    each = LANE // slots
    for t in range(topq):
        entry = slot_of[t : t + 1, :]
        owner = jnp.where(lax.div(entry, slots) == partition, 1.0, 0.0).astype(BF16)
        for h in range(half):
            answer_rows = jnp.zeros((LANE, sessions), F32)
            for piece in parts[h]:
                answer_rows = answer_rows + lax.dot_general(
                    piece, owner, (((0,), (0,)), ((), ())), preferred_element_type=F32
                )
            kept = jnp.where(lax.rem(entry, slots) == position, answer_rows, 0.0)
            for i in range(each):
                scores[pl.ds(t * nitems + h * each + i, 1), :] = jnp.sum(
                    kept[i * slots : (i + 1) * slots, :], axis=0, keepdims=True
                )


def body(
    features, send_rows, neighbours, w_self1, w_neigh1, w_self2, w_neigh2, queries, owners, slate
):
    ndom, nrep = lax.axis_size("dom"), lax.axis_size("rep")
    nx, nz = 4, 8
    nodes, width = features.shape
    fan = neighbours.shape[1]
    per_pair = send_rows.shape[1]
    chunk = nodes // nrep
    full = width * nrep
    sessions, topq, nitems = slate.shape
    capacity = min(sessions, 2 * sessions * topq // ndom)
    entries, nslots = sessions * topq, ndom * capacity
    count = capacity * nitems
    half = count // LANE
    qrows = capacity

    send_idx = send_rows.reshape(-1)
    neigh_idx = neighbours.T.reshape(-1)

    owner_of = owners.T.reshape(entries)
    named = owner_of[:, None] == jnp.arange(ndom, dtype=jnp.int32)[None, :]
    order = jnp.arange(entries, dtype=jnp.int32)
    earlier = (order[:, None] > order[None, :]).astype(BF16)
    before = jnp.dot(earlier, named.astype(BF16), preferred_element_type=F32)
    position = jnp.sum(jnp.where(named, before, 0.0), axis=1).astype(jnp.int32)
    slot_index = owner_of * capacity + position
    place = (jnp.arange(nslots, dtype=jnp.int32)[:, None] == slot_index[None, :]).astype(BF16)
    lists = slate.transpose(1, 0, 2).reshape(entries, nitems)
    digits = jnp.concatenate([lists // 64, lists % 64], axis=1).astype(BF16)
    slot_digits = jnp.dot(place, digits, preferred_element_type=F32).astype(jnp.int32)
    slot_lists = slot_digits[:, :nitems] * 64 + slot_digits[:, nitems:]
    slot_lists = slot_lists.reshape(ndom, capacity, nitems).transpose(0, 2, 1)
    slot_lists = slot_lists.reshape(ndom, half, LANE)

    dma = pltpu.SemaphoreType.DMA
    shape = jax.ShapeDtypeStruct
    whole = pl.BlockSpec(memory_space=VMEM)
    peers, others = (ndom - 1,), (nrep - 1,)
    args = [neigh_idx, send_idx, features, w_self1, w_neigh1, w_self2, w_neigh2, queries, slot_lists]
    args.append(slot_index.reshape(topq, sessions))
    per_layer = [dma((TILES, nrep - 1))] * 4 + [dma((2, TILES))]
    node_embed, scores = pl.pallas_call(
        functools.partial(kernel, nrep, ndom, nx, nz, fan, nitems),
        out_shape=[shape((nodes, width), BF16), shape((topq * nitems, sessions), F32)],
        in_specs=[pl.BlockSpec(memory_space=pltpu.SMEM)] * 2 + [whole] * (len(args) - 2),
        out_specs=[whole, whole],
        scratch_shapes=[
            VMEM((nodes + ndom * per_pair, width), F32),
            VMEM((chunk // TILES, width), F32),
            VMEM((per_pair, width), F32),
            VMEM((ndom * count, width), F32),
            VMEM((ndom * per_pair, width), BF16),
            VMEM((ndom * per_pair, width), BF16),
            VMEM((ndom * per_pair, width), BF16),
            VMEM((TILES, nrep, chunk // TILES, width), BF16),
            VMEM((TILES, nrep, chunk // TILES, width), BF16),
            VMEM((chunk, full), BF16),
            VMEM((chunk, full), BF16),
            VMEM((chunk, full), BF16),
            VMEM((chunk, full), BF16),
            VMEM((chunk, full), BF16),
            VMEM((nodes, width), BF16),
            VMEM((2 * full, full), BF16),
            VMEM((2 * full, full), BF16),
            VMEM((ndom * qrows, LANE), BF16),
            VMEM((ndom, half, LANE), jnp.int32),
            pltpu.SMEM((ndom, half, LANE), jnp.int32),
            VMEM((nrep, ndom, half, LANE), F32),
            VMEM((ndom, half, LANE), F32),
            VMEM((ndom, half, LANE), F32),
            VMEM((ndom * qrows, LANE), BF16),
        ]
        + [dma(peers)] * 10
        + [dma(others)] * 2
        + [dma((4, nrep - 1))] * 2
        + [dma(others)] * 2
        + per_layer
        + per_layer
        + [dma((9,))],
        compiler_params=pltpu.CompilerParams(
            collective_id=1, has_side_effects=True, vmem_limit_bytes=56 * 1024 * 1024
        ),
        name="graph_and_scores",
    )(*args)
    return (node_embed, scores.T)


def solution(mesh):
    placed = (
        P("dom", "rep"),
        P("dom", None),
        P("dom", None),
        P(None, "rep"),
        P(None, "rep"),
        P(None, "rep"),
        P(None, "rep"),
        P("dom", "rep"),
        P("dom", None),
        P("dom", None, None),
    )
    return jax.shard_map(
        body,
        mesh=mesh,
        in_specs=placed,
        out_specs=(P("dom", "rep"), P("dom", None)),
        check_vma=False,
    )
```

```python
import functools

import jax
import jax.numpy as jnp
from jax import lax
from jax.experimental import pallas as pl
from jax.experimental.pallas import tpu as pltpu
from jax.sharding import PartitionSpec as P

MESH = pl.DeviceIdType.MESH
VMEM = pltpu.VMEM
F32 = jnp.float32
BF16 = jnp.bfloat16
LANE = 128
EPS = 1e-06
TILES = 4
SHARES = 4


def columns_of(which):
    return pl.ds(pl.multiple_of(which * LANE, LANE), LANE)


def rows_of(which, count):
    return pl.ds(pl.multiple_of(which * count, count), count)


class Ring:
    def __init__(self, ndom, nx, nz):
        self.ndom, self.nx, self.nz = ndom, nx, nz
        me = lax.axis_index("dom")
        self.me = me
        self.core = lax.rem(me, 2)
        self.z = lax.rem(lax.div(me, 2), nz)
        self.x = lax.div(me, 2 * nz)

    def offset(self, n):
        nz, nx = self.nz, self.nx
        i = lax.rem(n, nz)
        dz = nz // 2 + (1 - 2 * lax.rem(i, 2)) * lax.div(i + 1, 2)
        turn = lax.div(n, nz)
        return lax.rem(lax.div(turn, 2) + 1, nx), dz, 1 - lax.rem(turn, 2)

    def target(self, n):
        dx, dz, dc = self.offset(n)
        x = lax.rem(self.x + dx, self.nx)
        z = lax.rem(self.z + dz, self.nz)
        return (x * self.nz + z) * 2 + lax.rem(self.core + dc, 2)

    def source(self, n):
        dx, dz, dc = self.offset(n)
        x = lax.rem(self.x - dx + self.nx, self.nx)
        z = lax.rem(self.z - dz + self.nz, self.nz)
        return (x * self.nz + z) * 2 + lax.rem(self.core + dc, 2)


def for_peers(ndom, me, act):
    peers = ndom - 1
    together = 7 if peers % 7 == 0 else 1

    def some(block, carry):
        for u in range(together):
            n = block * together + u
            act(n, lax.rem(me + 1 + n, ndom), lax.rem(me + ndom - 1 - n, ndom))
        return carry

    lax.fori_loop(0, peers // together, some, 0)


def to_dom(src, dst, send, recv, target):
    return pltpu.make_async_remote_copy(
        src_ref=src, dst_ref=dst, send_sem=send, recv_sem=recv,
        device_id={"dom": target}, device_id_type=MESH,
    )


def to_rep(src, dst, send, recv, target):
    return pltpu.make_async_remote_copy(
        src_ref=src, dst_ref=dst, send_sem=send, recv_sem=recv,
        device_id={"rep": target}, device_id_type=MESH,
    )


def pick_rows(index_of, table, stage, unroll):
    def some(block, carry):
        base = block * unroll
        for u in range(unroll):
            stage[pl.ds(base + u, 1), :] = table[pl.ds(index_of(base, u), 1), :]
        return carry

    lax.fori_loop(0, stage.shape[0] // unroll, some, 0)


def sum_rows(index_ref, start, table, stage, nodes, fan, unroll):
    span = nodes - unroll + 1

    def some(block, carry):
        base = block * unroll
        for u in range(unroll):
            terms = [
                table[pl.ds(index_ref.at[pl.ds(k * nodes + u, span)][start + base], 1), :]
                for k in range(fan)
            ]
            while len(terms) > 1:
                pairs = [terms[i] + terms[i + 1] for i in range(0, len(terms) - 1, 2)]
                terms = pairs + terms[len(pairs) * 2 :]
            stage[pl.ds(base + u, 1), :] = terms[0]
        return carry

    lax.fori_loop(0, stage.shape[0] // unroll, some, 0)


def start_boundary(ring, send_idx, table, nodes, pick, outgoing, landing, send, recv):
    count = pick.shape[0]

    def one(n, carry):
        to = ring.target(n)
        pick_rows(lambda base, u: send_idx[to * count + base + u], table, pick, 32)
        outgoing[rows_of(to, count), :] = pick[...].astype(BF16)
        to_dom(
            outgoing.at[rows_of(to, count), :],
            landing.at[rows_of(ring.me, count), :],
            send.at[n],
            recv.at[n],
            to,
        ).start()
        return carry

    lax.fori_loop(0, ring.ndom - 1, one, 0)
    me = ring.me
    pick_rows(lambda base, u: send_idx[me * count + base + u], table, pick, 32)
    table[pl.ds(pl.multiple_of(nodes + me * count, 64), count), :] = pick[...]


def finish_boundary(ring, table, nodes, count, outgoing, landing, send, recv):
    def one(n, carry):
        to, source = ring.target(n), ring.source(n)
        copy = to_dom(
            outgoing.at[rows_of(to, count), :],
            landing.at[rows_of(source, count), :],
            send.at[n],
            recv.at[n],
            to,
        )
        copy.wait_recv()
        table[pl.ds(pl.multiple_of(nodes + source * count, 64), count), :] = landing[
            rows_of(source, count), :
        ].astype(F32)
        copy.wait_send()
        return carry

    lax.fori_loop(0, ring.ndom - 1, one, 0)


def layer(
    active, me, nrep, fan, neigh_idx, nodes, table, stage, before_product,
    self_rows, weights, chunks, agg_rows, hid_rows, hid_cols, send, recv, hsend, hrecv, local,
):
    chunk = nodes // nrep
    width = self_rows.shape[1]
    tile = chunk // TILES

    def there(t):
        return agg_rows.at[pl.ds(t * tile, tile), columns_of(me)]

    def sum_copy(t, step):
        to = lax.rem(me + 1 + step, nrep)
        return to_rep(chunks.at[t, step], there(t), send.at[t, step], recv.at[t, step], to)

    def own_sum_copy(t):
        return pltpu.make_async_copy(chunks.at[t, nrep - 1], there(t), local.at[0, t])

    def sums(t):
        def summed(step):
            to = lax.rem(me + 1 + step, nrep)
            sum_rows(neigh_idx, to * chunk + t * tile, table, stage, nodes, fan, 32)
            chunks[t, step] = (stage[...] / fan).astype(BF16)

        def one(step, carry):
            summed(step)
            sum_copy(t, step).start()
            return carry

        lax.fori_loop(0, nrep - 1, one, 0)
        summed(nrep - 1)
        own_sum_copy(t).start()

    back = []

    def product(t):
        for step in range(nrep - 1):
            sum_copy(t, step).wait()
        own_sum_copy(t).wait()
        rows = pl.ds(t * tile, tile)
        z = jnp.dot(self_rows[rows, :], weights[pl.ds(0, width), :], preferred_element_type=F32)
        z = z + jnp.dot(
            agg_rows[rows, :], weights[pl.ds(width, width), :], preferred_element_type=F32
        )
        if active:
            z = jnp.maximum(z, 0.0)
        mean = jnp.sum(z * z, axis=1, keepdims=True) / width
        hid_rows[rows, :] = (z * lax.rsqrt(mean + EPS)).astype(BF16)
        landing = hid_cols.at[pl.ds(pl.multiple_of(me * chunk + t * tile, tile), tile), :]
        for step in range(nrep - 1):
            to = lax.rem(me + 1 + step, nrep)
            copy = to_rep(
                hid_rows.at[rows, columns_of(to)], landing, hsend.at[t, step], hrecv.at[t, step], to
            )
            copy.start()
            back.append(copy)
        copy = pltpu.make_async_copy(hid_rows.at[rows, columns_of(me)], landing, local.at[1, t])
        copy.start()
        back.append(copy)

    sums(0)
    for copy in before_product:
        copy.wait()
    for t in range(1, TILES):
        sums(t)
        product(t - 1)
    product(TILES - 1)
    for copy in back:
        copy.wait()
    table[pl.ds(0, nodes), :] = hid_cols[...].astype(F32)


def kernel(
    nrep, ndom, nx, nz, fan, nitems,
    neigh_idx, send_idx, own, wself1, wneigh1, wself2, wneigh2, queries, lists, slot_of,
    embed, scores,
    table, stage, pick, found, outgoing, landing1, landing2, chunks1, chunks2, agg1, agg2,
    x_rows, h_rows, e_rows, h_cols, weights1, weights2, got, got_lists, items, partial, total, fetched, asked,
    bsend1, brecv1, bsend2, brecv2, qsend, qrecv, isend, irecv, fsend, frecv, xsend, xrecv, wsend, wrecv,
    psend, precv, asend1, arecv1, hsend1, hrecv1, local1, asend2, arecv2, hsend2, hrecv2, local2,
    local,
):
    ring = Ring(ndom, nx, nz)
    me = lax.axis_index("rep")
    nodes = own.shape[0]
    chunk = nodes // nrep
    full = h_rows.shape[1]

    barrier = pltpu.get_barrier_semaphore()

    def greet(n, to, source):
        pl.semaphore_signal(barrier, inc=1, device_id={"dom": to}, device_id_type=MESH)

    for_peers(ndom, ring.me, greet)
    for step in range(1, nrep):
        pl.semaphore_signal(
            barrier, inc=1, device_id={"rep": lax.rem(me + step, nrep)}, device_id_type=MESH
        )
    table[pl.ds(0, nodes), :] = own[...].astype(F32)
    pl.semaphore_wait(barrier, ndom - 1 + nrep - 1)

    early = []
    blocks = (
        (wself1, weights1, 0), (wneigh1, weights1, full),
        (wself2, weights2, 0), (wneigh2, weights2, full),
    )
    for step in range(nrep - 1):
        to = lax.rem(me + 1 + step, nrep)
        early.append(
            to_rep(own.at[rows_of(to, chunk), :], x_rows.at[:, columns_of(me)],
                   xsend.at[step], xrecv.at[step], to)
        )
        for b, (part, whole, at) in enumerate(blocks):
            early.append(
                to_rep(part, whole.at[pl.ds(at, full), columns_of(me)],
                       wsend.at[b, step], wrecv.at[b, step], to)
            )
    early.append(
        pltpu.make_async_copy(own.at[rows_of(me, chunk), :], x_rows.at[:, columns_of(me)], local.at[0])
    )
    for b, (part, whole, at) in enumerate(blocks):
        early.append(
            pltpu.make_async_copy(part, whole.at[pl.ds(at, full), columns_of(me)], local.at[1 + b])
        )
    for copy in early:
        copy.start()

    count = pick.shape[0]
    start_boundary(ring, send_idx, table, nodes, pick, outgoing, landing1, bsend1, brecv1)
    sessions = queries.shape[0]
    topq = slot_of.shape[0]

    def fill(block, carry):
        slot = lax.broadcasted_iota(jnp.int32, (sessions, sessions), 0) + block * sessions
        rows = jnp.zeros((sessions, LANE), F32)
        for t in range(topq):
            place = jnp.where(slot_of[t : t + 1, :] == slot, 1.0, 0.0).astype(BF16)
            rows = rows + jnp.dot(place, queries[...], preferred_element_type=F32)
        asked[rows_of(block, sessions), :] = rows.astype(BF16)
        return carry

    lax.fori_loop(0, asked.shape[0] // sessions, fill, 0)
    finish_boundary(ring, table, nodes, count, outgoing, landing1, bsend1, brecv1)

    qrows = got.shape[0] // ndom
    own_asked = [
        pltpu.make_async_copy(
            asked.at[rows_of(ring.me, qrows), :], got.at[rows_of(ring.me, qrows), :],
            local.at[1 + len(blocks)],
        ),
        pltpu.make_async_copy(
            lists.at[ring.me], got_lists.at[ring.me], local.at[2 + len(blocks)]
        ),
    ]
    for copy in own_asked:
        copy.start()

    def query_copies(n, to, origin):
        return (
            to_dom(asked.at[rows_of(to, qrows), :], got.at[rows_of(origin, qrows), :],
                   qsend.at[n], qrecv.at[n], to),
            to_dom(lists.at[to], got_lists.at[origin], isend.at[n], irecv.at[n], to),
        )

    def ask(n, to, source):
        for copy in query_copies(n, to, ring.me):
            copy.start()

    for_peers(ndom, ring.me, ask)
    layer(
        True, me, nrep, fan, neigh_idx, nodes, table, stage, early, x_rows, weights1,
        chunks1, agg1, h_rows, h_cols, asend1, arecv1, hsend1, hrecv1, local1,
    )
    start_boundary(ring, send_idx, table, nodes, pick, outgoing, landing2, bsend2, brecv2)

    def asked_by(n, to, source):
        for copy in query_copies(n, to, source):
            copy.wait()

    for_peers(ndom, ring.me, asked_by)
    for copy in own_asked:
        copy.wait()
    into = pltpu.make_async_copy(got_lists, items, local.at[3 + len(blocks)])
    into.start()
    into.wait()
    finish_boundary(ring, table, nodes, count, outgoing, landing2, bsend2, brecv2)
    layer(
        False, me, nrep, fan, neigh_idx, nodes, table, stage, [], h_rows, weights2,
        chunks2, agg2, e_rows, embed, asend2, arecv2, hsend2, hrecv2, local2,
    )

    slots = qrows
    half = got_lists.shape[1]
    wide = half * LANE
    owns = lax.broadcasted_iota(jnp.int32, (slots, wide), 0)
    slot = lax.rem(lax.broadcasted_iota(jnp.int32, (slots, wide), 1), slots)

    def find(p, carry):
        base = pl.multiple_of(p * wide, wide)
        for h in range(half):
            for i in range(LANE):
                item = items.at[:, pl.ds(h, 1), pl.ds(i, 1)][p, 0, 0]
                found[pl.ds(base + (h * LANE + i), 1), :] = table[pl.ds(item, 1), :]
        return carry

    lax.fori_loop(0, ndom, find, 0)
    together = 4

    def score(block, carry):
        for u in range(together):
            p = block * together + u
            products = lax.dot_general(
                got[rows_of(p, slots), :],
                found[rows_of(p, wide), :].astype(BF16),
                (((1,), (1,)), ((), ())),
                preferred_element_type=F32,
            )
            kept = jnp.sum(jnp.where(owns == slot, products, 0.0), axis=0, keepdims=True)
            for h in range(half):
                partial[me, p, pl.ds(h, 1), :] = kept[:, h * LANE : (h + 1) * LANE]
        return carry

    steps = ndom // together // SHARES
    share = steps * together
    copies = []
    for b in range(SHARES):
        lax.fori_loop(b * steps, (b + 1) * steps, score, 0)
        mine = partial.at[me, pl.ds(b * share, share)]
        for step in range(nrep - 1):
            copy = to_rep(mine, mine, psend.at[b, step], precv.at[b, step],
                          lax.rem(me + 1 + step, nrep))
            copy.start()
            copies.append(copy)
    for copy in copies:
        copy.wait()
    added = partial[0]
    for other in range(1, nrep):
        added = added + partial[other]
    total[...] = added
    fetched[ring.me] = total[ring.me]

    def answer(n, to, source):
        to_dom(total.at[to], fetched.at[ring.me], fsend.at[n], frecv.at[n], to).start()

    def answered(n, to, source):
        to_dom(total.at[to], fetched.at[source], fsend.at[n], frecv.at[n], to).wait()

    for_peers(ndom, ring.me, answer)
    for_peers(ndom, ring.me, answered)

    parts = []
    for h in range(half):
        rest, split = fetched[:, h, :], []
        for _ in range(3):
            split.append(rest.astype(BF16))
            rest = rest - split[-1].astype(F32)
        parts.append(split)
    partition = lax.broadcasted_iota(jnp.int32, (ndom, sessions), 0)
    position = lax.rem(lax.broadcasted_iota(jnp.int32, (LANE, sessions), 0), slots)
    each = LANE // slots
    for t in range(topq):
        entry = slot_of[t : t + 1, :]
        owner = jnp.where(lax.div(entry, slots) == partition, 1.0, 0.0).astype(BF16)
        for h in range(half):
            answer_rows = jnp.zeros((LANE, sessions), F32)
            for piece in parts[h]:
                answer_rows = answer_rows + lax.dot_general(
                    piece, owner, (((0,), (0,)), ((), ())), preferred_element_type=F32
                )
            kept = jnp.where(lax.rem(entry, slots) == position, answer_rows, 0.0)
            for i in range(each):
                scores[pl.ds(t * nitems + h * each + i, 1), :] = jnp.sum(
                    kept[i * slots : (i + 1) * slots, :], axis=0, keepdims=True
                )


def body(
    features, send_rows, neighbours, w_self1, w_neigh1, w_self2, w_neigh2, queries, owners, slate
):
    ndom, nrep = lax.axis_size("dom"), lax.axis_size("rep")
    nx, nz = 4, 8
    nodes, width = features.shape
    fan = neighbours.shape[1]
    per_pair = send_rows.shape[1]
    chunk = nodes // nrep
    full = width * nrep
    sessions, topq, nitems = slate.shape
    capacity = min(sessions, 2 * sessions * topq // ndom)
    entries, nslots = sessions * topq, ndom * capacity
    count = capacity * nitems
    half = count // LANE
    qrows = capacity

    send_idx = send_rows.reshape(-1)
    neigh_idx = neighbours.T.reshape(-1)

    owner_of = owners.T.reshape(entries)
    named = owner_of[:, None] == jnp.arange(ndom, dtype=jnp.int32)[None, :]
    order = jnp.arange(entries, dtype=jnp.int32)
    earlier = (order[:, None] > order[None, :]).astype(BF16)
    before = jnp.dot(earlier, named.astype(BF16), preferred_element_type=F32)
    position = jnp.sum(jnp.where(named, before, 0.0), axis=1).astype(jnp.int32)
    slot_index = owner_of * capacity + position
    place = (jnp.arange(nslots, dtype=jnp.int32)[:, None] == slot_index[None, :]).astype(BF16)
    lists = slate.transpose(1, 0, 2).reshape(entries, nitems)
    digits = jnp.concatenate([lists // 64, lists % 64], axis=1).astype(BF16)
    slot_digits = jnp.dot(place, digits, preferred_element_type=F32).astype(jnp.int32)
    slot_lists = slot_digits[:, :nitems] * 64 + slot_digits[:, nitems:]
    slot_lists = slot_lists.reshape(ndom, capacity, nitems).transpose(0, 2, 1)
    slot_lists = slot_lists.reshape(ndom, half, LANE)

    dma = pltpu.SemaphoreType.DMA
    shape = jax.ShapeDtypeStruct
    whole = pl.BlockSpec(memory_space=VMEM)
    peers, others = (ndom - 1,), (nrep - 1,)
    args = [neigh_idx, send_idx, features, w_self1, w_neigh1, w_self2, w_neigh2, queries, slot_lists]
    args.append(slot_index.reshape(topq, sessions))
    per_layer = [dma((TILES, nrep - 1))] * 4 + [dma((2, TILES))]
    node_embed, scores = pl.pallas_call(
        functools.partial(kernel, nrep, ndom, nx, nz, fan, nitems),
        out_shape=[shape((nodes, width), BF16), shape((topq * nitems, sessions), F32)],
        in_specs=[pl.BlockSpec(memory_space=pltpu.SMEM)] * 2 + [whole] * (len(args) - 2),
        out_specs=[whole, whole],
        scratch_shapes=[
            VMEM((nodes + ndom * per_pair, width), F32),
            VMEM((chunk // TILES, width), F32),
            VMEM((per_pair, width), F32),
            VMEM((ndom * count, width), F32),
            VMEM((ndom * per_pair, width), BF16),
            VMEM((ndom * per_pair, width), BF16),
            VMEM((ndom * per_pair, width), BF16),
            VMEM((TILES, nrep, chunk // TILES, width), BF16),
            VMEM((TILES, nrep, chunk // TILES, width), BF16),
            VMEM((chunk, full), BF16),
            VMEM((chunk, full), BF16),
            VMEM((chunk, full), BF16),
            VMEM((chunk, full), BF16),
            VMEM((chunk, full), BF16),
            VMEM((nodes, width), BF16),
            VMEM((2 * full, full), BF16),
            VMEM((2 * full, full), BF16),
            VMEM((ndom * qrows, LANE), BF16),
            VMEM((ndom, half, LANE), jnp.int32),
            pltpu.SMEM((ndom, half, LANE), jnp.int32),
            VMEM((nrep, ndom, half, LANE), F32),
            VMEM((ndom, half, LANE), F32),
            VMEM((ndom, half, LANE), F32),
            VMEM((ndom * qrows, LANE), BF16),
        ]
        + [dma(peers)] * 10
        + [dma(others)] * 2
        + [dma((4, nrep - 1))] * 2
        + [dma((SHARES, nrep - 1))] * 2
        + per_layer
        + per_layer
        + [dma((9,))],
        compiler_params=pltpu.CompilerParams(
            collective_id=1, has_side_effects=True, vmem_limit_bytes=42 * 1024 * 1024
        ),
        name="graph_and_scores",
    )(*args)
    return (node_embed, scores.T)


def solution(mesh):
    placed = (
        P("dom", "rep"),
        P("dom", None),
        P("dom", None),
        P(None, "rep"),
        P(None, "rep"),
        P(None, "rep"),
        P(None, "rep"),
        P("dom", "rep"),
        P("dom", None),
        P("dom", None, None),
    )
    return jax.shard_map(
        body,
        mesh=mesh,
        in_specs=placed,
        out_specs=(P("dom", "rep"), P("dom", None)),
        check_vma=False,
    )
```

```python
import functools

import jax
import jax.numpy as jnp
from jax import lax
from jax.experimental import pallas as pl
from jax.experimental.pallas import tpu as pltpu
from jax.sharding import PartitionSpec as P

MESH = pl.DeviceIdType.MESH
VMEM = pltpu.VMEM
F32 = jnp.float32
BF16 = jnp.bfloat16
LANE = 128
EPS = 1e-06
TILES = 4
SHARES = 4


def columns_of(which):
    return pl.ds(pl.multiple_of(which * LANE, LANE), LANE)


def rows_of(which, count):
    return pl.ds(pl.multiple_of(which * count, count), count)


class Ring:
    def __init__(self, ndom, nx, nz):
        self.ndom, self.nx, self.nz = ndom, nx, nz
        me = lax.axis_index("dom")
        self.me = me
        self.core = lax.rem(me, 2)
        self.z = lax.rem(lax.div(me, 2), nz)
        self.x = lax.div(me, 2 * nz)

    def offset(self, n):
        nz, nx = self.nz, self.nx
        i = lax.rem(n, nz)
        dz = nz // 2 + (1 - 2 * lax.rem(i, 2)) * lax.div(i + 1, 2)
        turn = lax.div(n, nz)
        return lax.rem(lax.div(turn, 2) + 1, nx), dz, 1 - lax.rem(turn, 2)

    def target(self, n):
        dx, dz, dc = self.offset(n)
        x = lax.rem(self.x + dx, self.nx)
        z = lax.rem(self.z + dz, self.nz)
        return (x * self.nz + z) * 2 + lax.rem(self.core + dc, 2)

    def source(self, n):
        dx, dz, dc = self.offset(n)
        x = lax.rem(self.x - dx + self.nx, self.nx)
        z = lax.rem(self.z - dz + self.nz, self.nz)
        return (x * self.nz + z) * 2 + lax.rem(self.core + dc, 2)


def for_peers(ndom, me, act):
    peers = ndom - 1
    together = 7 if peers % 7 == 0 else 1

    def some(block, carry):
        for u in range(together):
            n = block * together + u
            act(n, lax.rem(me + 1 + n, ndom), lax.rem(me + ndom - 1 - n, ndom))
        return carry

    lax.fori_loop(0, peers // together, some, 0)


def to_dom(src, dst, send, recv, target):
    return pltpu.make_async_remote_copy(
        src_ref=src, dst_ref=dst, send_sem=send, recv_sem=recv,
        device_id={"dom": target}, device_id_type=MESH,
    )


def to_rep(src, dst, send, recv, target):
    return pltpu.make_async_remote_copy(
        src_ref=src, dst_ref=dst, send_sem=send, recv_sem=recv,
        device_id={"rep": target}, device_id_type=MESH,
    )


def pick_rows(index_of, table, stage, unroll):
    def some(block, carry):
        base = block * unroll
        for u in range(unroll):
            stage[pl.ds(base + u, 1), :] = table[pl.ds(index_of(base, u), 1), :]
        return carry

    lax.fori_loop(0, stage.shape[0] // unroll, some, 0)


def sum_rows(index_ref, start, table, stage, nodes, fan, unroll):
    span = nodes - unroll + 1

    def some(block, carry):
        base = block * unroll
        for u in range(unroll):
            terms = [
                table[pl.ds(index_ref.at[pl.ds(k * nodes + u, span)][start + base], 1), :]
                for k in range(fan)
            ]
            while len(terms) > 1:
                pairs = [terms[i] + terms[i + 1] for i in range(0, len(terms) - 1, 2)]
                terms = pairs + terms[len(pairs) * 2 :]
            stage[pl.ds(base + u, 1), :] = terms[0]
        return carry

    lax.fori_loop(0, stage.shape[0] // unroll, some, 0)


def start_boundary(ring, send_idx, table, nodes, pick, outgoing, landing, send, recv):
    count = pick.shape[0]
    span = ring.ndom * count - 31

    def one(n, carry):
        to = ring.target(n)
        pick_rows(lambda base, u: send_idx.at[pl.ds(u, span)][to * count + base], table, pick, 32)
        outgoing[rows_of(to, count), :] = pick[...].astype(BF16)
        to_dom(
            outgoing.at[rows_of(to, count), :],
            landing.at[rows_of(ring.me, count), :],
            send.at[n],
            recv.at[n],
            to,
        ).start()
        return carry

    lax.fori_loop(0, ring.ndom - 1, one, 0)
    me = ring.me
    pick_rows(lambda base, u: send_idx.at[pl.ds(u, span)][me * count + base], table, pick, 32)
    table[pl.ds(pl.multiple_of(nodes + me * count, 64), count), :] = pick[...]


def finish_boundary(ring, table, nodes, count, outgoing, landing, send, recv):
    def one(n, carry):
        to, source = ring.target(n), ring.source(n)
        copy = to_dom(
            outgoing.at[rows_of(to, count), :],
            landing.at[rows_of(source, count), :],
            send.at[n],
            recv.at[n],
            to,
        )
        copy.wait_recv()
        table[pl.ds(pl.multiple_of(nodes + source * count, 64), count), :] = landing[
            rows_of(source, count), :
        ].astype(F32)
        copy.wait_send()
        return carry

    lax.fori_loop(0, ring.ndom - 1, one, 0)


def layer(
    active, me, nrep, fan, neigh_idx, nodes, table, stage, before_product,
    self_rows, weights, chunks, agg_rows, hid_rows, hid_cols, send, recv, hsend, hrecv, local,
):
    chunk = nodes // nrep
    width = self_rows.shape[1]
    tile = chunk // TILES

    def there(t):
        return agg_rows.at[pl.ds(t * tile, tile), columns_of(me)]

    def sum_copy(t, step):
        to = lax.rem(me + 1 + step, nrep)
        return to_rep(chunks.at[t, step], there(t), send.at[t, step], recv.at[t, step], to)

    def own_sum_copy(t):
        return pltpu.make_async_copy(chunks.at[t, nrep - 1], there(t), local.at[0, t])

    def sums(t):
        def summed(step):
            to = lax.rem(me + 1 + step, nrep)
            sum_rows(neigh_idx, to * chunk + t * tile, table, stage, nodes, fan, 32)
            chunks[t, step] = (stage[...] / fan).astype(BF16)

        def one(step, carry):
            summed(step)
            sum_copy(t, step).start()
            return carry

        lax.fori_loop(0, nrep - 1, one, 0)
        summed(nrep - 1)
        own_sum_copy(t).start()

    back = []

    def product(t):
        for step in range(nrep - 1):
            sum_copy(t, step).wait()
        own_sum_copy(t).wait()
        rows = pl.ds(t * tile, tile)
        z = jnp.dot(self_rows[rows, :], weights[pl.ds(0, width), :], preferred_element_type=F32)
        z = z + jnp.dot(
            agg_rows[rows, :], weights[pl.ds(width, width), :], preferred_element_type=F32
        )
        if active:
            z = jnp.maximum(z, 0.0)
        mean = jnp.sum(z * z, axis=1, keepdims=True) / width
        hid_rows[rows, :] = (z * lax.rsqrt(mean + EPS)).astype(BF16)
        landing = hid_cols.at[pl.ds(pl.multiple_of(me * chunk + t * tile, tile), tile), :]
        for step in range(nrep - 1):
            to = lax.rem(me + 1 + step, nrep)
            copy = to_rep(
                hid_rows.at[rows, columns_of(to)], landing, hsend.at[t, step], hrecv.at[t, step], to
            )
            copy.start()
            back.append(copy)
        copy = pltpu.make_async_copy(hid_rows.at[rows, columns_of(me)], landing, local.at[1, t])
        copy.start()
        back.append(copy)

    sums(0)
    for copy in before_product:
        copy.wait()
    for t in range(1, TILES):
        sums(t)
        product(t - 1)
    product(TILES - 1)
    for copy in back:
        copy.wait()
    table[pl.ds(0, nodes), :] = hid_cols[...].astype(F32)


def kernel(
    nrep, ndom, nx, nz, fan, nitems,
    neigh_idx, send_idx, own, wself1, wneigh1, wself2, wneigh2, queries, lists, slot_of,
    embed, scores,
    table, stage, pick, found, outgoing, landing1, landing2, chunks1, chunks2, agg1, agg2,
    x_rows, h_rows, e_rows, h_cols, weights1, weights2, got, got_lists, items, partial, total, fetched, asked,
    bsend1, brecv1, bsend2, brecv2, qsend, qrecv, isend, irecv, fsend, frecv, xsend, xrecv, wsend, wrecv,
    psend, precv, asend1, arecv1, hsend1, hrecv1, local1, asend2, arecv2, hsend2, hrecv2, local2,
    local,
):
    ring = Ring(ndom, nx, nz)
    me = lax.axis_index("rep")
    nodes = own.shape[0]
    chunk = nodes // nrep
    full = h_rows.shape[1]

    barrier = pltpu.get_barrier_semaphore()

    def greet(n, to, source):
        pl.semaphore_signal(barrier, inc=1, device_id={"dom": to}, device_id_type=MESH)

    for_peers(ndom, ring.me, greet)
    for step in range(1, nrep):
        pl.semaphore_signal(
            barrier, inc=1, device_id={"rep": lax.rem(me + step, nrep)}, device_id_type=MESH
        )
    table[pl.ds(0, nodes), :] = own[...].astype(F32)
    pl.semaphore_wait(barrier, ndom - 1 + nrep - 1)

    early = []
    blocks = (
        (wself1, weights1, 0), (wneigh1, weights1, full),
        (wself2, weights2, 0), (wneigh2, weights2, full),
    )
    for step in range(nrep - 1):
        to = lax.rem(me + 1 + step, nrep)
        early.append(
            to_rep(own.at[rows_of(to, chunk), :], x_rows.at[:, columns_of(me)],
                   xsend.at[step], xrecv.at[step], to)
        )
        for b, (part, whole, at) in enumerate(blocks):
            early.append(
                to_rep(part, whole.at[pl.ds(at, full), columns_of(me)],
                       wsend.at[b, step], wrecv.at[b, step], to)
            )
    early.append(
        pltpu.make_async_copy(own.at[rows_of(me, chunk), :], x_rows.at[:, columns_of(me)], local.at[0])
    )
    for b, (part, whole, at) in enumerate(blocks):
        early.append(
            pltpu.make_async_copy(part, whole.at[pl.ds(at, full), columns_of(me)], local.at[1 + b])
        )
    for copy in early:
        copy.start()

    count = pick.shape[0]
    start_boundary(ring, send_idx, table, nodes, pick, outgoing, landing1, bsend1, brecv1)
    sessions = queries.shape[0]
    topq = slot_of.shape[0]

    def fill(block, carry):
        slot = lax.broadcasted_iota(jnp.int32, (sessions, sessions), 0) + block * sessions
        rows = jnp.zeros((sessions, LANE), F32)
        for t in range(topq):
            place = jnp.where(slot_of[t : t + 1, :] == slot, 1.0, 0.0).astype(BF16)
            rows = rows + jnp.dot(place, queries[...], preferred_element_type=F32)
        asked[rows_of(block, sessions), :] = rows.astype(BF16)
        return carry

    lax.fori_loop(0, asked.shape[0] // sessions, fill, 0)
    finish_boundary(ring, table, nodes, count, outgoing, landing1, bsend1, brecv1)

    qrows = got.shape[0] // ndom
    own_asked = [
        pltpu.make_async_copy(
            asked.at[rows_of(ring.me, qrows), :], got.at[rows_of(ring.me, qrows), :],
            local.at[1 + len(blocks)],
        ),
        pltpu.make_async_copy(
            lists.at[ring.me], got_lists.at[ring.me], local.at[2 + len(blocks)]
        ),
    ]
    for copy in own_asked:
        copy.start()

    def query_copies(n, to, origin):
        return (
            to_dom(asked.at[rows_of(to, qrows), :], got.at[rows_of(origin, qrows), :],
                   qsend.at[n], qrecv.at[n], to),
            to_dom(lists.at[to], got_lists.at[origin], isend.at[n], irecv.at[n], to),
        )

    def ask(n, to, source):
        for copy in query_copies(n, to, ring.me):
            copy.start()

    for_peers(ndom, ring.me, ask)
    layer(
        True, me, nrep, fan, neigh_idx, nodes, table, stage, early, x_rows, weights1,
        chunks1, agg1, h_rows, h_cols, asend1, arecv1, hsend1, hrecv1, local1,
    )
    start_boundary(ring, send_idx, table, nodes, pick, outgoing, landing2, bsend2, brecv2)

    def asked_by(n, to, source):
        for copy in query_copies(n, to, source):
            copy.wait()

    for_peers(ndom, ring.me, asked_by)
    for copy in own_asked:
        copy.wait()
    into = pltpu.make_async_copy(got_lists, items, local.at[3 + len(blocks)])
    into.start()
    into.wait()
    finish_boundary(ring, table, nodes, count, outgoing, landing2, bsend2, brecv2)
    layer(
        False, me, nrep, fan, neigh_idx, nodes, table, stage, [], h_rows, weights2,
        chunks2, agg2, e_rows, embed, asend2, arecv2, hsend2, hrecv2, local2,
    )

    slots = qrows
    half = got_lists.shape[1]
    wide = half * LANE
    owns = lax.broadcasted_iota(jnp.int32, (slots, wide), 0)
    slot = lax.rem(lax.broadcasted_iota(jnp.int32, (slots, wide), 1), slots)

    def find(p, carry):
        base = pl.multiple_of(p * wide, wide)
        for h in range(half):
            for i in range(LANE):
                item = items.at[:, pl.ds(h, 1), pl.ds(i, 1)][p, 0, 0]
                found[pl.ds(base + (h * LANE + i), 1), :] = table[pl.ds(item, 1), :]
        return carry

    lax.fori_loop(0, ndom, find, 0)
    together = 4

    def score(block, carry):
        for u in range(together):
            p = block * together + u
            products = lax.dot_general(
                got[rows_of(p, slots), :],
                found[rows_of(p, wide), :].astype(BF16),
                (((1,), (1,)), ((), ())),
                preferred_element_type=F32,
            )
            kept = jnp.sum(jnp.where(owns == slot, products, 0.0), axis=0, keepdims=True)
            for h in range(half):
                partial[me, p, pl.ds(h, 1), :] = kept[:, h * LANE : (h + 1) * LANE]
        return carry

    steps = ndom // together // SHARES
    share = steps * together
    copies = []
    for b in range(SHARES):
        lax.fori_loop(b * steps, (b + 1) * steps, score, 0)
        mine = partial.at[me, pl.ds(b * share, share)]
        for step in range(nrep - 1):
            copy = to_rep(mine, mine, psend.at[b, step], precv.at[b, step],
                          lax.rem(me + 1 + step, nrep))
            copy.start()
            copies.append(copy)
    for copy in copies:
        copy.wait()
    added = partial[0]
    for other in range(1, nrep):
        added = added + partial[other]
    total[...] = added
    fetched[ring.me] = total[ring.me]

    def answer(n, to, source):
        to_dom(total.at[to], fetched.at[ring.me], fsend.at[n], frecv.at[n], to).start()

    def answered(n, to, source):
        to_dom(total.at[to], fetched.at[source], fsend.at[n], frecv.at[n], to).wait()

    for_peers(ndom, ring.me, answer)
    for_peers(ndom, ring.me, answered)

    parts = []
    for h in range(half):
        rest, split = fetched[:, h, :], []
        for _ in range(3):
            split.append(rest.astype(BF16))
            rest = rest - split[-1].astype(F32)
        parts.append(split)
    partition = lax.broadcasted_iota(jnp.int32, (ndom, sessions), 0)
    position = lax.rem(lax.broadcasted_iota(jnp.int32, (LANE, sessions), 0), slots)
    each = LANE // slots
    for t in range(topq):
        entry = slot_of[t : t + 1, :]
        owner = jnp.where(lax.div(entry, slots) == partition, 1.0, 0.0).astype(BF16)
        for h in range(half):
            answer_rows = jnp.zeros((LANE, sessions), F32)
            for piece in parts[h]:
                answer_rows = answer_rows + lax.dot_general(
                    piece, owner, (((0,), (0,)), ((), ())), preferred_element_type=F32
                )
            kept = jnp.where(lax.rem(entry, slots) == position, answer_rows, 0.0)
            for i in range(each):
                scores[pl.ds(t * nitems + h * each + i, 1), :] = jnp.sum(
                    kept[i * slots : (i + 1) * slots, :], axis=0, keepdims=True
                )


def body(
    features, send_rows, neighbours, w_self1, w_neigh1, w_self2, w_neigh2, queries, owners, slate
):
    ndom, nrep = lax.axis_size("dom"), lax.axis_size("rep")
    nx, nz = 4, 8
    nodes, width = features.shape
    fan = neighbours.shape[1]
    per_pair = send_rows.shape[1]
    chunk = nodes // nrep
    full = width * nrep
    sessions, topq, nitems = slate.shape
    capacity = min(sessions, 2 * sessions * topq // ndom)
    entries, nslots = sessions * topq, ndom * capacity
    count = capacity * nitems
    half = count // LANE
    qrows = capacity

    send_idx = send_rows.reshape(-1)
    neigh_idx = neighbours.T.reshape(-1)

    owner_of = owners.T.reshape(entries)
    named = owner_of[:, None] == jnp.arange(ndom, dtype=jnp.int32)[None, :]
    order = jnp.arange(entries, dtype=jnp.int32)
    earlier = (order[:, None] > order[None, :]).astype(BF16)
    before = jnp.dot(earlier, named.astype(BF16), preferred_element_type=F32)
    position = jnp.sum(jnp.where(named, before, 0.0), axis=1).astype(jnp.int32)
    slot_index = owner_of * capacity + position
    place = (jnp.arange(nslots, dtype=jnp.int32)[:, None] == slot_index[None, :]).astype(BF16)
    lists = slate.transpose(1, 0, 2).reshape(entries, nitems)
    digits = jnp.concatenate([lists // 64, lists % 64], axis=1).astype(BF16)
    slot_digits = jnp.dot(place, digits, preferred_element_type=F32).astype(jnp.int32)
    slot_lists = slot_digits[:, :nitems] * 64 + slot_digits[:, nitems:]
    slot_lists = slot_lists.reshape(ndom, capacity, nitems).transpose(0, 2, 1)
    slot_lists = slot_lists.reshape(ndom, half, LANE)

    dma = pltpu.SemaphoreType.DMA
    shape = jax.ShapeDtypeStruct
    whole = pl.BlockSpec(memory_space=VMEM)
    peers, others = (ndom - 1,), (nrep - 1,)
    args = [neigh_idx, send_idx, features, w_self1, w_neigh1, w_self2, w_neigh2, queries, slot_lists]
    args.append(slot_index.reshape(topq, sessions))
    per_layer = [dma((TILES, nrep - 1))] * 4 + [dma((2, TILES))]
    node_embed, scores = pl.pallas_call(
        functools.partial(kernel, nrep, ndom, nx, nz, fan, nitems),
        out_shape=[shape((nodes, width), BF16), shape((topq * nitems, sessions), F32)],
        in_specs=[pl.BlockSpec(memory_space=pltpu.SMEM)] * 2 + [whole] * (len(args) - 2),
        out_specs=[whole, whole],
        scratch_shapes=[
            VMEM((nodes + ndom * per_pair, width), F32),
            VMEM((chunk // TILES, width), F32),
            VMEM((per_pair, width), F32),
            VMEM((ndom * count, width), F32),
            VMEM((ndom * per_pair, width), BF16),
            VMEM((ndom * per_pair, width), BF16),
            VMEM((ndom * per_pair, width), BF16),
            VMEM((TILES, nrep, chunk // TILES, width), BF16),
            VMEM((TILES, nrep, chunk // TILES, width), BF16),
            VMEM((chunk, full), BF16),
            VMEM((chunk, full), BF16),
            VMEM((chunk, full), BF16),
            VMEM((chunk, full), BF16),
            VMEM((chunk, full), BF16),
            VMEM((nodes, width), BF16),
            VMEM((2 * full, full), BF16),
            VMEM((2 * full, full), BF16),
            VMEM((ndom * qrows, LANE), BF16),
            VMEM((ndom, half, LANE), jnp.int32),
            pltpu.SMEM((ndom, half, LANE), jnp.int32),
            VMEM((nrep, ndom, half, LANE), F32),
            VMEM((ndom, half, LANE), F32),
            VMEM((ndom, half, LANE), F32),
            VMEM((ndom * qrows, LANE), BF16),
        ]
        + [dma(peers)] * 10
        + [dma(others)] * 2
        + [dma((4, nrep - 1))] * 2
        + [dma((SHARES, nrep - 1))] * 2
        + per_layer
        + per_layer
        + [dma((9,))],
        compiler_params=pltpu.CompilerParams(
            collective_id=1, has_side_effects=True, vmem_limit_bytes=42 * 1024 * 1024
        ),
        name="graph_and_scores",
    )(*args)
    return (node_embed, scores.T)


def solution(mesh):
    placed = (
        P("dom", "rep"),
        P("dom", None),
        P("dom", None),
        P(None, "rep"),
        P(None, "rep"),
        P(None, "rep"),
        P(None, "rep"),
        P("dom", "rep"),
        P("dom", None),
        P("dom", None, None),
    )
    return jax.shard_map(
        body,
        mesh=mesh,
        in_specs=placed,
        out_specs=(P("dom", "rep"), P("dom", None)),
        check_vma=False,
    )
```
